512 devices in a mesh: dp: 2 (over core), seq: 64 (over y, z_hi, x), head: 4 (over z_lo).
Axes of the slice: x: 4, y: 4, z: 16 (z_hi: 4, z_lo: 4; z = z_hi * 4 + z_lo), core: 2. Of those that a mesh axis runs over, the one named last changes fastest.
Arguments:
- frames: bfloat16 [2, 49152, 1536], P('dp', ('seq', 'head')), may hold values from -600 to 600
- norm_gain: float32 [1536], replicated, may hold values from 0.1 to 1.9
- w_query: bfloat16 [1536, 1536], P('dp', 'head'), may hold values from -1.6 to 1.6
- w_key: bfloat16 [1536, 1536], P('dp', 'head'), may hold values from -16 to 16
- w_value: bfloat16 [1536, 1536], P('dp', 'head'), may hold values from -0.15625 to 0.15625
- w_out: bfloat16 [1536, 1536], P('head', 'dp'), may hold values from -0.4375 to 0.4375
- group_band: int32 [2, 384, 12], P('dp', 'seq'), may hold values 0 or 1
- lengths: int32 [2], P('dp'), may hold values from 24576 to 49152
Outputs:
- update: bfloat16 [2, 49152, 1536], P('dp', ('seq', 'head'))
The draws below stay inside these ranges and needn't reach their ends.
All inputs are finite; a program needn't handle non-finite values. No bound on the sum of `group_band` on one device may be relied on, other than what follows from the above.
Results may differ from the reference program's by a relative error of at most 0.012.
Values may be sent and summed in bfloat16 or wider, within the bound.
A program may use at most 128 MiB of HBM per device.

```python
import math
import jax
import jax.numpy as jnp
from jax import lax

D = 1536
HEADS = 24
HD = 64
GROUP = 128
BATCH = 2
FRAMES = 49152
GROUP_DEV = 6
GROUPS = 384


def query_base(key):
    return jnp.clip(jax.random.normal(jax.random.fold_in(key, 11), (D, HEADS * HD), jnp.float32), -6.0, 6.0)


def draw_frames(key, part):
    key = jax.random.fold_in(key, 3)
    noise_key, row_key, col_key = jax.random.split(key, 3)
    row_scale = jnp.exp(jax.random.uniform(row_key, (BATCH, FRAMES, 1), jnp.float32, 0.0, math.log(10.0)))
    col_scale = jnp.exp(jax.random.uniform(col_key, (1, 1, D), jnp.float32, 0.0, math.log(10.0)))
    values = jnp.clip(jax.random.normal(noise_key, (BATCH, FRAMES, D), jnp.float32), -6.0, 6.0)
    return (values * row_scale * col_scale).astype(jnp.bfloat16)


def draw_w_query(key, part):
    return (query_base(key) * (2.0 / math.sqrt(D))).astype(jnp.bfloat16)


def draw_w_key(key, part):
    key = jax.random.fold_in(key, 7)
    noise_key = jax.random.fold_in(key, 0)
    noise = jnp.clip(jax.random.normal(noise_key, (D, HEADS * HD), jnp.float32), -6.0, 6.0) / math.sqrt(D)
    values = noise
    return values.astype(jnp.bfloat16)


def with_ends(result, own_key, low, largest):
    spot = [jax.random.randint(jax.random.fold_in(own_key, axis), (), 0, length) for axis, length in enumerate(result.shape)]
    longest = result.shape.index(max(result.shape))
    next_to = spot[:longest] + [(spot[longest] + 1) % result.shape[longest]] + spot[longest + 1:]
    return result.at[tuple(spot)].set(low).at[tuple(next_to)].set(largest)


def block_scale(own_key, shape, cuts, smallest, largest):
    def one(dim, shards_of):
        heights = jax.random.uniform(jax.random.fold_in(jax.random.fold_in(own_key, 6), dim), (shards_of,), jnp.float32, smallest / len(cuts), largest / len(cuts))
        return jnp.repeat(jnp.exp(heights), shape[dim] // shards_of).reshape((-1,) + (1,) * (len(shape) - dim - 1))

    level = one(*cuts[0])
    for cut in cuts[1:]:
        level = level * one(*cut)
    return level


def gaussian(key, shape, deviation, most, cuts=(), held_as=jnp.bfloat16):
    drawn = jax.random.normal(key, shape, jnp.float32) * deviation
    if len(cuts) > 0:
        drawn = block_scale(key, shape, cuts, -0.22, 0.18) * drawn
    return jnp.clip(drawn, min=-most, max=most).astype(held_as)


def setup_inputs(seed: int = 0) -> dict:
    key_list = jax.random.split(jax.random.key(seed), 9)
    frames = draw_frames(jax.random.fold_in(key_list[8], 71), 0)
    norm_gain = jnp.clip(1.0 + 0.18 * jax.random.normal(key_list[1], (D,), jnp.float32), 0.1, 1.9)
    w_query = draw_w_query(jax.random.fold_in(key_list[8], 71), 0)
    w_key = draw_w_key(jax.random.fold_in(key_list[8], 71), 0)
    w_value = gaussian(key_list[4], (D, HEADS * HD), D ** -0.5, 0.15625, ((0, 2), (1, 4)))
    w_out = gaussian(key_list[5], (HEADS * HD, D), (D // 8) ** -0.5, 0.4375, ((0, 4), (1, 2)))
    group_band = with_ends((jax.random.randint(key_list[6], (BATCH, GROUPS, 2 * GROUP_DEV), 0, 2) < 1).astype(jnp.int32), jax.random.fold_in(key_list[6], 1), 0, 1)
    lengths = jax.random.randint(key_list[7], (BATCH,), FRAMES // 2, FRAMES + 1).astype(jnp.int32)
    return dict(frames=frames, norm_gain=norm_gain, w_query=w_query, w_key=w_key, w_value=w_value, w_out=w_out, group_band=group_band, lengths=lengths)


epsilon = 1e-05

def layer_norm(rows, norm_gain):
    values = rows.astype(jnp.float32)
    center = values - lax.optimization_barrier(jnp.mean(values, axis=-1, keepdims=True))
    spread = lax.optimization_barrier(jnp.mean(center * center, axis=-1, keepdims=True))
    return (center * lax.rsqrt(spread + epsilon) * norm_gain.astype(jnp.float32)).astype(jnp.bfloat16)

def permission(query_start, key_start, query_groups, key_groups, group_size, band_rows, length_value, total_groups):
    query_ids = query_start + jnp.arange(query_groups, dtype=jnp.int32)
    key_ids = key_start + jnp.arange(key_groups, dtype=jnp.int32)
    offsets = key_ids[None, :] - query_ids[:, None]
    reach_groups = band_rows.shape[1] // 2
    column = jnp.where(offsets < 0, offsets + reach_groups, offsets + reach_groups - 1)
    hits = column[:, :, None] == jnp.arange(2 * reach_groups, dtype=jnp.int32)[None, None, :]
    picked = lax.optimization_barrier(jnp.sum(jnp.where(hits, band_rows[:, None, :], 0), axis=-1))
    inside = (key_ids >= 0) & (key_ids < total_groups)
    linked = (offsets != 0) & (jnp.abs(offsets) <= reach_groups) & inside[None, :] & (picked == 1)
    key_frames = key_start * group_size + jnp.arange(key_groups * group_size, dtype=jnp.int32)
    alive_keys = key_frames < length_value
    linked_rows = jnp.repeat(jnp.repeat(linked, group_size, axis=0), group_size, axis=1) & alive_keys[None, :]
    same_group = jnp.repeat(jnp.repeat(offsets == 0, group_size, axis=0), group_size, axis=1)
    return linked_rows | same_group

def utterance(frames_one, norm_gain, w_query, w_key, w_value, w_out, band_one, length_value):
    normalized = layer_norm(frames_one, norm_gain)
    queries = jnp.dot(normalized, w_query, preferred_element_type=jnp.float32).astype(jnp.bfloat16)
    keys_all = jnp.dot(normalized, w_key, preferred_element_type=jnp.float32).astype(jnp.bfloat16)
    values_all = jnp.dot(normalized, w_value, preferred_element_type=jnp.float32).astype(jnp.bfloat16)
    block_rows = GROUP_DEV * GROUP
    margin = jnp.zeros((block_rows, HEADS * HD), jnp.bfloat16)
    keys_padded = jnp.concatenate([margin, keys_all, margin], axis=0)
    values_padded = jnp.concatenate([margin, values_all, margin], axis=0)
    score_scale = 1.0 / math.sqrt(HD)

    def block_context(block_index):
        first_row = block_index * block_rows
        query_block = lax.dynamic_slice_in_dim(queries, first_row, block_rows, 0).astype(jnp.float32).reshape(block_rows, HEADS, HD)
        key_block = lax.dynamic_slice_in_dim(keys_padded, first_row, 3 * block_rows, 0).astype(jnp.float32).reshape(3 * block_rows, HEADS, HD)
        value_block = lax.dynamic_slice_in_dim(values_padded, first_row, 3 * block_rows, 0).astype(jnp.float32).reshape(3 * block_rows, HEADS, HD)
        band_block = lax.dynamic_slice_in_dim(band_one, block_index * GROUP_DEV, GROUP_DEV, 0)
        allowed = permission(block_index * GROUP_DEV, block_index * GROUP_DEV - GROUP_DEV, GROUP_DEV, 3 * GROUP_DEV, GROUP, band_block, length_value, GROUPS)
        scores = jnp.einsum('qhd,khd->hqk', query_block, key_block) * score_scale
        masked = jnp.where(allowed[None, :, :], scores, -jnp.inf)
        row_max = lax.optimization_barrier(jnp.max(masked, axis=-1, keepdims=True))
        weights = jnp.exp(masked - row_max)
        row_total = lax.optimization_barrier(jnp.sum(weights, axis=-1, keepdims=True))
        rounded = lax.optimization_barrier(weights.astype(jnp.bfloat16)).astype(jnp.float32)
        context = jnp.einsum('hqk,khd->hqd', rounded, value_block) / row_total
        return jnp.transpose(context, (1, 0, 2)).reshape(block_rows, HEADS * HD).astype(jnp.bfloat16)
    contexts = lax.map(block_context, jnp.arange(GROUPS // GROUP_DEV, dtype=jnp.int32))
    context = contexts.reshape(FRAMES, HEADS * HD)
    return jnp.dot(context, w_out, preferred_element_type=jnp.float32).astype(jnp.bfloat16)

def reference(frames, norm_gain, w_query, w_key, w_value, w_out, group_band, lengths):
    updates = [utterance(frames[utter_index], norm_gain, w_query, w_key, w_value, w_out, group_band[utter_index], lengths[utter_index]) for utter_index in range(BATCH)]
    return jnp.stack(updates, axis=0)
```

```python
import functools

import jax
import jax.numpy as jnp
from jax import lax
from jax.experimental import pallas as pl
from jax.experimental.pallas import tpu as pltpu
from jax.sharding import PartitionSpec as P

MESH = pl.DeviceIdType.MESH
HD = 64
GROUP = 128
ROWS = 192
RUN = 768
WIDTH = 384
D = 1536
REACH = 6
PIECE = 48
QB = 256
FORBIDDEN = -1e30
epsilon = 1e-05


def kernel(
    frames, gain, w_query, w_key, w_value, band, lengths, out,
    weights, normalized, query, kv, bias, onehot, acc, top, context, gathered, relay_up, relay_down,
    w_send, w_recv, w_local, left_send, right_send, block_recv,
    up_send, up_recv, down_send, down_recv,
    spread_up_send, spread_up_recv, spread_down_send, spread_down_recv,
    far_up_send, far_up_recv, far_down_send, far_down_recv,
    ctx_send, ctx_recv,
):
    dp, seq, head = lax.axis_index("dp"), lax.axis_index("seq"), lax.axis_index("head")
    row, x = seq // 4, seq % 4
    first_seq = row * 4
    has_up, has_down = row < 15, row > 0

    def copy(src, dst, send, recv, to):
        return pltpu.make_async_remote_copy(
            src_ref=src, dst_ref=dst, send_sem=send, recv_sem=recv, device_id=to, device_id_type=MESH
        )

    barrier = pltpu.get_barrier_semaphore()

    def greet(to):
        pl.semaphore_signal(barrier, inc=1, device_id=to, device_id_type=MESH)

    greet((1 - dp, seq, head))
    for k in (1, 2, 3):
        greet((dp, seq, (head + k) % 4))
        greet((dp, first_seq + (x + k) % 4, head))

    @pl.when((x == 0) & has_down)
    def _():
        for q in range(4):
            greet((dp, first_seq - 4 + q, head))

    @pl.when((x == 3) & has_up)
    def _():
        for q in range(4):
            greet((dp, first_seq + 4 + q, head))

    pl.semaphore_wait(barrier, 7 + (1 - (row + 1) // 16) + (row + 15) // 16)

    half = pl.ds(pl.multiple_of(dp * (D // 2), D // 2), D // 2)

    def weight_there(i, ref):
        part = weights.at[half, pl.ds(i * WIDTH, WIDTH)]
        return copy(ref, part, w_send.at[i], w_recv.at[i], (1 - dp, seq, head))

    def weight_here(i, ref):
        return pltpu.make_async_copy(ref, weights.at[half, pl.ds(i * WIDTH, WIDTH)], w_local.at[i])

    for i, ref in enumerate((w_query, w_key, w_value)):
        weight_there(i, ref).start()
        weight_here(i, ref).start()

    values = frames[...].astype(jnp.float32)
    center = values - jnp.mean(values, axis=-1, keepdims=True)
    spread = jnp.mean(center * center, axis=-1, keepdims=True)
    normalized[head] = (center * lax.rsqrt(spread + epsilon) * gain[...]).astype(jnp.bfloat16)

    has_left, has_right = head > 0, head < 3
    left = (dp, seq, (head + 3) % 4)
    right = (dp, seq, (head + 1) % 4)

    def to_left(b):
        return copy(normalized.at[b], normalized.at[b], left_send.at[b], block_recv.at[b], left)

    def to_right(b):
        return copy(normalized.at[b], normalized.at[b], right_send.at[b], block_recv.at[b], right)

    pl.when(has_left)(lambda: to_left(head).start())
    pl.when(has_right)(lambda: to_right(head).start())

    onehot[...] = (
        lax.broadcasted_iota(jnp.int32, (RUN, 128), 0) // GROUP
        == lax.broadcasted_iota(jnp.int32, (RUN, 128), 1)
    ).astype(jnp.bfloat16)
    lane = lax.broadcasted_iota(jnp.int32, (1, 128), 1)
    within = lax.broadcasted_iota(jnp.int32, (GROUP, 128), 0)
    for kg in range(3 * REACH):
        seen = jnp.zeros((1, 128), jnp.int32)
        own = jnp.zeros((1, 128), jnp.int32)
        for g in range(REACH):
            offset = kg - REACH - g
            if offset == 0:
                own = jnp.where(lane == g, 1, own)
            elif abs(offset) <= REACH:
                column = offset + REACH if offset < 0 else offset + REACH - 1
                seen = jnp.where(lane == g, band[g, column], seen)
        group = seq * REACH - REACH + kg
        inside = jnp.where((group >= 0) & (group < 64 * REACH), 1, 0)
        alive = (group * GROUP + within < lengths[0]).astype(jnp.int32) * inside
        allowed = (jnp.where(seen == 1, 1, 0) * alive + own) > 0
        bias[kg * GROUP:(kg + 1) * GROUP, :] = jnp.where(allowed, 0.0, FORBIDDEN).astype(jnp.bfloat16)

    @pl.when(seq == 0)
    def _():
        kv[0:RUN, :] = jnp.zeros((RUN, 2 * WIDTH), jnp.bfloat16)

    @pl.when(seq == 63)
    def _():
        kv[2 * RUN:3 * RUN, :] = jnp.zeros((RUN, 2 * WIDTH), jnp.bfloat16)

    for i, ref in enumerate((w_query, w_key, w_value)):
        weight_here(i, ref).wait()
        weight_there(i, ref).wait_recv()

    def place(side, b, q=None):
        start, size = side * RUN + b * ROWS, ROWS
        if q is not None:
            start, size = start + q * PIECE, PIECE
        return kv.at[pl.ds(pl.multiple_of(start, 16), size), :]

    def up_near(b):
        return copy(place(1, b), place(0, b), up_send.at[b], up_recv.at[b], (dp, (seq + 1) % 64, head))

    def down_near(b):
        return copy(place(1, b), place(2, b), down_send.at[b], down_recv.at[b], (dp, (seq + 63) % 64, head))

    def up_spread(b, q):
        return copy(
            place(1, b, q), relay_up.at[b], spread_up_send.at[b, q], spread_up_recv.at[b], (dp, first_seq + q, head)
        )

    def down_spread(b, q):
        return copy(
            place(1, b, q), relay_down.at[b], spread_down_send.at[b, q], spread_down_recv.at[b],
            (dp, first_seq + q, head),
        )

    def up_far(b, src, q):
        return copy(src, place(0, b, q), far_up_send.at[b], far_up_recv.at[b, q], (dp, (first_seq + 4) % 64, head))

    def down_far(b, src, q):
        return copy(src, place(2, b, q), far_down_send.at[b], far_down_recv.at[b, q], (dp, (first_seq + 63) % 64, head))

    sends_up_far, sends_down_far = (x == 3) & has_up, (x == 0) & has_down
    relays_up, relays_down = (x < 3) & has_up, (x > 0) & has_down

    def send_block(b):
        pl.when(x < 3)(lambda: up_near(b).start())
        pl.when(x > 0)(lambda: down_near(b).start())

        @pl.when(sends_up_far)
        def _():
            for q in range(3):
                up_spread(b, q).start()
            up_far(b, place(1, b, 3), 3).start()

        @pl.when(sends_down_far)
        def _():
            for q in range(1, 4):
                down_spread(b, q).start()
            down_far(b, place(1, b, 0), 0).start()

    def relay_block(b):
        @pl.when(relays_up)
        def _():
            up_spread(b, x).wait_recv()
            up_far(b, relay_up.at[b], x).start()

        @pl.when(relays_down)
        def _():
            down_spread(b, x).wait_recv()
            down_far(b, relay_down.at[b], x).start()

    far_end = head // 2
    mirrored = head + far_end * (3 - 2 * head)

    def nth(t):
        near = t // 2 * 2 + (t + mirrored * (1 - t // 2)) % 2
        return near + far_end * (3 - 2 * near)

    def project(t, carry):
        b = nth(t)

        @pl.when(t > 0)
        def _():
            to_left(b).wait_recv()
            pl.when((b < head) & has_right)(lambda: to_right(b).start())
            pl.when((b > head) & has_left)(lambda: to_left(b).start())

        rows = normalized[b]
        product = jnp.dot(rows, weights[...], preferred_element_type=jnp.float32).astype(jnp.bfloat16)
        start = pl.multiple_of(b * ROWS, ROWS)
        query[pl.ds(start, ROWS), :] = product[:, :WIDTH] * jnp.bfloat16(0.125)
        kv[pl.ds(pl.multiple_of(RUN + start, ROWS), ROWS), :] = product[:, WIDTH:]
        send_block(b)
        pl.when(t > 0)(lambda: relay_block(nth((t + 3) % 4)))
        return carry

    lax.fori_loop(0, 4, project, 0)

    low_half = lax.broadcasted_iota(jnp.int32, (QB, 128), 1) < HD

    def attend(p, query_start, key_start, keys, first):
        lanes = pl.ds(pl.multiple_of(p * 128, 128), 128)
        value_lanes = pl.ds(pl.multiple_of(WIDTH + p * 128, 128), 128)
        key_rows = pl.ds(pl.multiple_of(key_start, QB), keys)
        query_rows = pl.ds(pl.multiple_of(query_start, QB), QB)
        key_tile = jnp.concatenate([kv[key_rows, lanes], bias[key_rows, :]], axis=1)
        value_tile = jnp.concatenate([kv[key_rows, value_lanes], jnp.ones((keys, 128), jnp.bfloat16)], axis=1)
        query_tile = query[query_rows, lanes]
        marks = onehot[query_rows, :]
        for hh in range(2):
            h = p * 2 + hh
            mine = jnp.where(low_half == (hh == 0), query_tile, jnp.zeros_like(query_tile))
            scores = lax.dot_general(
                jnp.concatenate([mine, marks], axis=1), key_tile, (((1,), (1,)), ((), ())),
                preferred_element_type=jnp.float32,
            )
            here = jnp.max(scores, axis=-1, keepdims=True)
            if first:
                best = here
            else:
                before = top[h, query_rows, :][:, :1]
                best = jnp.maximum(before, here)
            rounded = jnp.exp(scores - best).astype(jnp.bfloat16)
            part = jnp.dot(rounded, value_tile, preferred_element_type=jnp.float32)
            if not first:
                part = part + acc[h, query_rows, :] * jnp.exp(before - best)
            acc[h, query_rows, :] = part
            top[h, query_rows, :] = jnp.broadcast_to(best, (QB, 128))

    def own_part(p, carry):
        for j in range(3):
            attend(p, j * QB, RUN, RUN, True)
        pl.when(p == 0)(lambda: relay_block(nth(3)))
        return carry

    lax.fori_loop(0, 3, own_part, 0)

    def wait_side(side):
        @pl.when(side == 0)
        def _():
            @pl.when(x > 0)
            def _():
                for b in range(4):
                    up_near(b).wait_recv()

            @pl.when((x == 0) & has_down)
            def _():
                for b in range(4):
                    for q in range(4):
                        up_far(b, place(1, b, q), q).wait_recv()

        @pl.when(side == 1)
        def _():
            @pl.when(x < 3)
            def _():
                for b in range(4):
                    down_near(b).wait_recv()

            @pl.when((x == 3) & has_up)
            def _():
                for b in range(4):
                    for q in range(4):
                        down_far(b, place(1, b, q), q).wait_recv()

    def side_part(p, side):
        for j in range(3):
            query_start = j * QB + side * (2 * QB - 2 * j * QB)
            key_start = j * QB + side * (2 * RUN - j * QB)
            attend(p, query_start, key_start, RUN - j * QB, False)

    first_side = 1 - (x + 3) // 4
    wait_side(first_side)

    def early_part(p, carry):
        side_part(p, first_side)
        return carry

    lax.fori_loop(0, 3, early_part, 0)
    last_side = 1 - first_side
    wait_side(last_side)

    def ctx_copy(p, k):
        to = (head + k) % 4
        return copy(
            context.at[pl.ds(pl.multiple_of(to * ROWS, ROWS), ROWS), pl.ds(pl.multiple_of(p * 128, 128), 128)],
            gathered.at[:, pl.ds(pl.multiple_of(head * WIDTH + p * 128, 128), 128)],
            ctx_send.at[p, k - 1], ctx_recv.at[p, k - 1], (dp, seq, to),
        )

    def late_part(p, carry):
        side_part(p, last_side)
        lanes = pl.ds(pl.multiple_of(p * 128, 128), 128)
        for j in range(3):
            rows = pl.ds(j * QB, QB)
            low, high = acc[p * 2, rows, :], acc[p * 2 + 1, rows, :]
            context[rows, lanes] = jnp.where(
                low_half, low[:, :128] / low[:, 128:], high[:, :128] / high[:, 128:]
            ).astype(jnp.bfloat16)
        for k in (2, 1, 3):
            ctx_copy(p, k).start()
        return carry

    lax.fori_loop(0, 3, late_part, 0)
    own_lanes = pl.ds(pl.multiple_of(head * WIDTH, 128), WIDTH)
    gathered[:, own_lanes] = context[pl.ds(pl.multiple_of(head * ROWS, ROWS), ROWS), :]

    for i, ref in enumerate((w_query, w_key, w_value)):
        weight_there(i, ref).wait_send()
    for b in range(4):
        pl.when((b <= head) & has_right)(lambda: to_right(b).wait_send())
        pl.when((b >= head) & has_left)(lambda: to_left(b).wait_send())
        pl.when(x < 3)(lambda: up_near(b).wait_send())
        pl.when(x > 0)(lambda: down_near(b).wait_send())

        @pl.when(sends_up_far)
        def _():
            for q in range(3):
                up_spread(b, q).wait_send()

        @pl.when(sends_down_far)
        def _():
            for q in range(1, 4):
                down_spread(b, q).wait_send()

        pl.when(has_up)(lambda: up_far(b, place(1, b, 3), 3).wait_send())
        pl.when(has_down)(lambda: down_far(b, place(1, b, 0), 0).wait_send())
    for p in range(3):
        for k in (1, 2, 3):
            ctx_copy(p, k).wait()
    out[...] = gathered[...]


def exchange_and_attend(frames, gain, w_query, w_key, w_value, band, lengths):
    vmem, smem, anywhere = (pl.BlockSpec(memory_space=m) for m in (pltpu.VMEM, pltpu.SMEM, pl.ANY))
    dma = pltpu.SemaphoreType.DMA
    bf16, f32 = jnp.bfloat16, jnp.float32
    return pl.pallas_call(
        kernel,
        out_shape=jax.ShapeDtypeStruct((ROWS, D), bf16),
        in_specs=[vmem, vmem, anywhere, anywhere, anywhere, smem, smem],
        out_specs=vmem,
        scratch_shapes=[
            pltpu.VMEM((D, 3 * WIDTH), bf16),
            pltpu.VMEM((4, ROWS, D), bf16),
            pltpu.VMEM((RUN, WIDTH), bf16),
            pltpu.VMEM((3 * RUN, 2 * WIDTH), bf16),
            pltpu.VMEM((3 * RUN, 128), bf16),
            pltpu.VMEM((RUN, 128), bf16),
            pltpu.VMEM((6, RUN, 256), f32),
            pltpu.VMEM((6, RUN, 128), f32),
            pltpu.VMEM((RUN, WIDTH), bf16),
            pltpu.VMEM((ROWS, D), bf16),
            pltpu.VMEM((4, PIECE, 2 * WIDTH), bf16),
            pltpu.VMEM((4, PIECE, 2 * WIDTH), bf16),
            dma((3,)), dma((3,)), dma((3,)),
            dma((4,)), dma((4,)), dma((4,)),
            dma((4,)), dma((4,)), dma((4,)), dma((4,)),
            dma((4, 4)), dma((4,)), dma((4, 4)), dma((4,)),
            dma((4,)), dma((4, 4)), dma((4,)), dma((4, 4)),
            dma((3, 3)), dma((3, 3)),
        ],
        compiler_params=pltpu.CompilerParams(
            collective_id=0, has_side_effects=True, vmem_limit_bytes=48 * 2**20
        ),
        cost_estimate=pl.CostEstimate(flops=60_000_000_000, bytes_accessed=8_000_000, transcendentals=8_000_000),
        name="attend",
    )(frames, gain, w_query, w_key, w_value, band, lengths)


def local(frames, norm_gain, w_query, w_key, w_value, w_out, group_band, lengths):
    frame_context = exchange_and_attend(
        frames[0], norm_gain[None], w_query, w_key, w_value, group_band[0], lengths
    )
    full_rows = lax.all_gather(w_out, "head", axis=0, tiled=True)
    update = jnp.dot(
        frame_context,
        lax.all_gather(full_rows, "dp", axis=1, tiled=True),
        preferred_element_type=jnp.float32,
    )
    return update.astype(jnp.bfloat16)[None]


def solution(mesh):
    return jax.shard_map(
        local,
        mesh=mesh,
        in_specs=(
            P("dp", ("seq", "head"), None),
            P(),
            P("dp", "head"),
            P("dp", "head"),
            P("dp", "head"),
            P("head", "dp"),
            P("dp", "seq", None),
            P("dp"),
        ),
        out_specs=P("dp", ("seq", "head"), None),
        check_vma=False,
    )
```

```python
import functools

import jax
import jax.numpy as jnp
from jax import lax
from jax.experimental import pallas as pl
from jax.experimental.pallas import tpu as pltpu
from jax.sharding import PartitionSpec as P

MESH = pl.DeviceIdType.MESH
HD = 64
GROUP = 128
ROWS = 192
RUN = 768
WIDTH = 384
D = 1536
REACH = 6
PIECE = 48
QB = 256
FORBIDDEN = -1e30
epsilon = 1e-05


def kernel(
    frames, gain, w_query, w_key, w_value, w_out, band, lengths, out,
    weights, normalized, query, kv, bias, onehot, acc, top, context, gathered, relay_up, relay_down, projection,
    w_send, w_recv, w_local, left_send, right_send, block_recv,
    up_send, up_recv, down_send, down_recv,
    spread_up_send, spread_up_recv, spread_down_send, spread_down_recv,
    far_up_send, far_up_recv, far_down_send, far_down_recv,
    ctx_send, ctx_recv,
    out_local, out_z_send, out_z_recv, out_x_send, out_x_recv, out_y_send, out_y_recv, out_core_send, out_core_recv,
):
    dp, seq, head = lax.axis_index("dp"), lax.axis_index("seq"), lax.axis_index("head")
    row, x = seq // 4, seq % 4
    y = seq // 16
    first_seq = row * 4
    has_up, has_down = row < 15, row > 0

    def copy(src, dst, send, recv, to):
        return pltpu.make_async_remote_copy(
            src_ref=src, dst_ref=dst, send_sem=send, recv_sem=recv, device_id=to, device_id_type=MESH
        )

    barrier = pltpu.get_barrier_semaphore()

    def greet(to):
        pl.semaphore_signal(barrier, inc=1, device_id=to, device_id_type=MESH)

    greet((1 - dp, seq, head))
    for k in (1, 2, 3):
        greet((dp, seq, (head + k) % 4))
        greet((dp, first_seq + (x + k) % 4, head))
        greet((dp, (seq + 16 * k) % 64, head))

    @pl.when((x == 0) & has_down)
    def _():
        for q in range(4):
            greet((dp, first_seq - 4 + q, head))

    @pl.when((x == 3) & has_up)
    def _():
        for q in range(4):
            greet((dp, first_seq + 4 + q, head))

    pl.semaphore_wait(barrier, 10 + (1 - (row + 1) // 16) + (row + 15) // 16)

    half = pl.ds(pl.multiple_of(dp * (D // 2), D // 2), D // 2)

    def weight_there(i, ref):
        part = weights.at[half, pl.ds(i * WIDTH, WIDTH)]
        return copy(ref, part, w_send.at[i], w_recv.at[i], (1 - dp, seq, head))

    def weight_here(i, ref):
        return pltpu.make_async_copy(ref, weights.at[half, pl.ds(i * WIDTH, WIDTH)], w_local.at[i])

    for i, ref in enumerate((w_query, w_key, w_value)):
        weight_there(i, ref).start()
        weight_here(i, ref).start()

    piece_rows = pl.ds(pl.multiple_of(y * 96 + x % 2 * 48, 16), 48)
    strip_rows = pl.ds(pl.multiple_of(y * 96, 16), 96)
    piece_from = pl.ds(pl.multiple_of(x // 2 * WIDTH, 128), WIDTH)
    piece_columns = pl.ds(pl.multiple_of(dp * (D // 2) + x // 2 * WIDTH, 128), WIDTH)

    def out_here():
        return pltpu.make_async_copy(
            w_out.at[piece_rows, piece_from], projection.at[head, piece_rows, piece_columns], out_local
        )

    def out_z(k):
        return copy(
            w_out.at[piece_rows, piece_from], projection.at[head, piece_rows, piece_columns],
            out_z_send.at[k - 1], out_z_recv.at[k - 1], (dp, seq, (head + k) % 4),
        )

    def out_x(k):
        part = projection.at[:, piece_rows, piece_columns]
        return copy(part, part, out_x_send.at[k - 1], out_x_recv.at[k - 1], (dp, first_seq + (x + k) % 4, head))

    def out_y(k):
        part = projection.at[:, strip_rows, half]
        return copy(part, part, out_y_send.at[k - 1], out_y_recv.at[k - 1], (dp, (seq + 16 * k) % 64, head))

    def out_core():
        part = projection.at[:, :, half]
        return copy(part, part, out_core_send, out_core_recv, (1 - dp, seq, head))

    out_here().start()
    for k in (2, 1, 3):
        out_z(k).start()

    values = frames[...].astype(jnp.float32)
    center = values - jnp.mean(values, axis=-1, keepdims=True)
    spread = jnp.mean(center * center, axis=-1, keepdims=True)
    normalized[head] = (center * lax.rsqrt(spread + epsilon) * gain[...]).astype(jnp.bfloat16)

    has_left, has_right = head > 0, head < 3
    left = (dp, seq, (head + 3) % 4)
    right = (dp, seq, (head + 1) % 4)

    def to_left(b):
        return copy(normalized.at[b], normalized.at[b], left_send.at[b], block_recv.at[b], left)

    def to_right(b):
        return copy(normalized.at[b], normalized.at[b], right_send.at[b], block_recv.at[b], right)

    pl.when(has_left)(lambda: to_left(head).start())
    pl.when(has_right)(lambda: to_right(head).start())

    onehot[...] = (
        lax.broadcasted_iota(jnp.int32, (RUN, 128), 0) // GROUP
        == lax.broadcasted_iota(jnp.int32, (RUN, 128), 1)
    ).astype(jnp.bfloat16)
    lane = lax.broadcasted_iota(jnp.int32, (1, 128), 1)
    within = lax.broadcasted_iota(jnp.int32, (GROUP, 128), 0)
    for kg in range(3 * REACH):
        seen = jnp.zeros((1, 128), jnp.int32)
        own = jnp.zeros((1, 128), jnp.int32)
        for g in range(REACH):
            offset = kg - REACH - g
            if offset == 0:
                own = jnp.where(lane == g, 1, own)
            elif abs(offset) <= REACH:
                column = offset + REACH if offset < 0 else offset + REACH - 1
                seen = jnp.where(lane == g, band[g, column], seen)
        group = seq * REACH - REACH + kg
        inside = jnp.where((group >= 0) & (group < 64 * REACH), 1, 0)
        alive = (group * GROUP + within < lengths[0]).astype(jnp.int32) * inside
        allowed = (jnp.where(seen == 1, 1, 0) * alive + own) > 0
        bias[kg * GROUP:(kg + 1) * GROUP, :] = jnp.where(allowed, 0.0, FORBIDDEN).astype(jnp.bfloat16)

    @pl.when(seq == 0)
    def _():
        kv[0:RUN, :] = jnp.zeros((RUN, 2 * WIDTH), jnp.bfloat16)

    @pl.when(seq == 63)
    def _():
        kv[2 * RUN:3 * RUN, :] = jnp.zeros((RUN, 2 * WIDTH), jnp.bfloat16)

    for i, ref in enumerate((w_query, w_key, w_value)):
        weight_here(i, ref).wait()
        weight_there(i, ref).wait_recv()

    def place(side, b, q=None):
        start, size = side * RUN + b * ROWS, ROWS
        if q is not None:
            start, size = start + q * PIECE, PIECE
        return kv.at[pl.ds(pl.multiple_of(start, 16), size), :]

    def up_near(b):
        return copy(place(1, b), place(0, b), up_send.at[b], up_recv.at[b], (dp, (seq + 1) % 64, head))

    def down_near(b):
        return copy(place(1, b), place(2, b), down_send.at[b], down_recv.at[b], (dp, (seq + 63) % 64, head))

    def up_spread(b, q):
        return copy(
            place(1, b, q), relay_up.at[b], spread_up_send.at[b, q], spread_up_recv.at[b], (dp, first_seq + q, head)
        )

    def down_spread(b, q):
        return copy(
            place(1, b, q), relay_down.at[b], spread_down_send.at[b, q], spread_down_recv.at[b],
            (dp, first_seq + q, head),
        )

    def up_far(b, src, q):
        return copy(src, place(0, b, q), far_up_send.at[b], far_up_recv.at[b, q], (dp, (first_seq + 4) % 64, head))

    def down_far(b, src, q):
        return copy(src, place(2, b, q), far_down_send.at[b], far_down_recv.at[b, q], (dp, (first_seq + 63) % 64, head))

    sends_up_far, sends_down_far = (x == 3) & has_up, (x == 0) & has_down
    relays_up, relays_down = (x < 3) & has_up, (x > 0) & has_down

    def send_block(b):
        pl.when(x < 3)(lambda: up_near(b).start())
        pl.when(x > 0)(lambda: down_near(b).start())

        @pl.when(sends_up_far)
        def _():
            for q in range(3):
                up_spread(b, q).start()
            up_far(b, place(1, b, 3), 3).start()

        @pl.when(sends_down_far)
        def _():
            for q in range(1, 4):
                down_spread(b, q).start()
            down_far(b, place(1, b, 0), 0).start()

    def relay_block(b):
        @pl.when(relays_up)
        def _():
            up_spread(b, x).wait_recv()
            up_far(b, relay_up.at[b], x).start()

        @pl.when(relays_down)
        def _():
            down_spread(b, x).wait_recv()
            down_far(b, relay_down.at[b], x).start()

    far_end = head // 2
    mirrored = head + far_end * (3 - 2 * head)

    def nth(t):
        near = t // 2 * 2 + (t + mirrored * (1 - t // 2)) % 2
        return near + far_end * (3 - 2 * near)

    def project(t, carry):
        b = nth(t)

        @pl.when(t > 0)
        def _():
            to_left(b).wait_recv()
            pl.when((b < head) & has_right)(lambda: to_right(b).start())
            pl.when((b > head) & has_left)(lambda: to_left(b).start())

        @pl.when(t == 1)
        def _():
            out_here().wait()
            for k in (1, 2, 3):
                out_z(k).wait_recv()
            for k in (2, 1, 3):
                out_x(k).start()

        @pl.when(t == 2 + mirrored)
        def _():
            for k in (1, 2, 3):
                out_x(k).wait_recv()
            for k in (2, 1, 3):
                out_y(k).start()

        rows = normalized[b]
        product = jnp.dot(rows, weights[...], preferred_element_type=jnp.float32).astype(jnp.bfloat16)
        start = pl.multiple_of(b * ROWS, ROWS)
        query[pl.ds(start, ROWS), :] = product[:, :WIDTH] * jnp.bfloat16(0.125)
        kv[pl.ds(pl.multiple_of(RUN + start, ROWS), ROWS), :] = product[:, WIDTH:]
        send_block(b)
        pl.when(t > 0)(lambda: relay_block(nth((t + 3) % 4)))
        return carry

    lax.fori_loop(0, 4, project, 0)

    low_half = lax.broadcasted_iota(jnp.int32, (QB, 128), 1) < HD

    def attend(p, query_start, key_start, keys, first):
        lanes = pl.ds(pl.multiple_of(p * 128, 128), 128)
        value_lanes = pl.ds(pl.multiple_of(WIDTH + p * 128, 128), 128)
        key_rows = pl.ds(pl.multiple_of(key_start, QB), keys)
        query_rows = pl.ds(pl.multiple_of(query_start, QB), QB)
        key_tile = jnp.concatenate([kv[key_rows, lanes], bias[key_rows, :]], axis=1)
        value_tile = jnp.concatenate([kv[key_rows, value_lanes], jnp.ones((keys, 128), jnp.bfloat16)], axis=1)
        query_tile = query[query_rows, lanes]
        marks = onehot[query_rows, :]
        for hh in range(2):
            h = p * 2 + hh
            mine = jnp.where(low_half == (hh == 0), query_tile, jnp.zeros_like(query_tile))
            scores = lax.dot_general(
                jnp.concatenate([mine, marks], axis=1), key_tile, (((1,), (1,)), ((), ())),
                preferred_element_type=jnp.float32,
            )
            here = jnp.max(scores, axis=-1, keepdims=True)
            if first:
                best = here
            else:
                before = top[h, query_rows, :][:, :1]
                best = jnp.maximum(before, here)
            rounded = jnp.exp(scores - best).astype(jnp.bfloat16)
            part = jnp.dot(rounded, value_tile, preferred_element_type=jnp.float32)
            if not first:
                part = part + acc[h, query_rows, :] * jnp.exp(before - best)
            acc[h, query_rows, :] = part
            top[h, query_rows, :] = jnp.broadcast_to(best, (QB, 128))

    def own_part(p, carry):
        for j in range(3):
            attend(p, j * QB, RUN, RUN, True)
        pl.when(p == 0)(lambda: relay_block(nth(3)))
        return carry

    lax.fori_loop(0, 3, own_part, 0)

    def wait_side(side):
        @pl.when(side == 0)
        def _():
            @pl.when(x > 0)
            def _():
                for b in range(4):
                    up_near(b).wait_recv()

            @pl.when((x == 0) & has_down)
            def _():
                for b in range(4):
                    for q in range(4):
                        up_far(b, place(1, b, q), q).wait_recv()

        @pl.when(side == 1)
        def _():
            @pl.when(x < 3)
            def _():
                for b in range(4):
                    down_near(b).wait_recv()

            @pl.when((x == 3) & has_up)
            def _():
                for b in range(4):
                    for q in range(4):
                        down_far(b, place(1, b, q), q).wait_recv()

    def side_part(p, side):
        for j in range(3):
            query_start = j * QB + side * (2 * QB - 2 * j * QB)
            key_start = j * QB + side * (2 * RUN - j * QB)
            attend(p, query_start, key_start, RUN - j * QB, False)

    first_side = 1 - (x + 3) // 4
    wait_side(first_side)

    def early_part(p, carry):
        side_part(p, first_side)
        return carry

    lax.fori_loop(0, 3, early_part, 0)
    for k in (1, 2, 3):
        out_y(k).wait_recv()
    out_core().start()
    last_side = 1 - first_side
    wait_side(last_side)

    def ctx_copy(p, k):
        to = (head + k) % 4
        return copy(
            context.at[pl.ds(pl.multiple_of(to * ROWS, ROWS), ROWS), pl.ds(pl.multiple_of(p * 128, 128), 128)],
            gathered.at[:, pl.ds(pl.multiple_of(head * WIDTH + p * 128, 128), 128)],
            ctx_send.at[p, k - 1], ctx_recv.at[p, k - 1], (dp, seq, to),
        )

    def late_part(p, carry):
        side_part(p, last_side)
        lanes = pl.ds(pl.multiple_of(p * 128, 128), 128)
        for j in range(3):
            rows = pl.ds(j * QB, QB)
            low, high = acc[p * 2, rows, :], acc[p * 2 + 1, rows, :]
            context[rows, lanes] = jnp.where(
                low_half, low[:, :128] / low[:, 128:], high[:, :128] / high[:, 128:]
            ).astype(jnp.bfloat16)
        for k in (2, 1, 3):
            ctx_copy(p, k).start()
        return carry

    lax.fori_loop(0, 3, late_part, 0)
    own_lanes = pl.ds(pl.multiple_of(head * WIDTH, 128), WIDTH)
    gathered[:, own_lanes] = context[pl.ds(pl.multiple_of(head * ROWS, ROWS), ROWS), :]

    for i, ref in enumerate((w_query, w_key, w_value)):
        weight_there(i, ref).wait_send()
    for b in range(4):
        pl.when((b <= head) & has_right)(lambda: to_right(b).wait_send())
        pl.when((b >= head) & has_left)(lambda: to_left(b).wait_send())
        pl.when(x < 3)(lambda: up_near(b).wait_send())
        pl.when(x > 0)(lambda: down_near(b).wait_send())

        @pl.when(sends_up_far)
        def _():
            for q in range(3):
                up_spread(b, q).wait_send()

        @pl.when(sends_down_far)
        def _():
            for q in range(1, 4):
                down_spread(b, q).wait_send()

        pl.when(has_up)(lambda: up_far(b, place(1, b, 3), 3).wait_send())
        pl.when(has_down)(lambda: down_far(b, place(1, b, 0), 0).wait_send())
    for k in (1, 2, 3):
        out_z(k).wait_send()
        out_x(k).wait_send()
        out_y(k).wait_send()
    out_core().wait()
    for p in range(3):
        for k in (1, 2, 3):
            ctx_copy(p, k).wait()
    total = jnp.dot(gathered[:, :WIDTH], projection[0], preferred_element_type=jnp.float32)
    for g in range(1, 4):
        total += jnp.dot(
            gathered[:, g * WIDTH:(g + 1) * WIDTH], projection[g], preferred_element_type=jnp.float32
        )
    out[...] = total.astype(jnp.bfloat16)


def exchange_and_attend(frames, gain, w_query, w_key, w_value, band, lengths, w_out):
    vmem, smem, anywhere = (pl.BlockSpec(memory_space=m) for m in (pltpu.VMEM, pltpu.SMEM, pl.ANY))
    dma = pltpu.SemaphoreType.DMA
    bf16, f32 = jnp.bfloat16, jnp.float32
    return pl.pallas_call(
        kernel,
        out_shape=jax.ShapeDtypeStruct((ROWS, D), bf16),
        in_specs=[vmem, vmem, anywhere, anywhere, anywhere, anywhere, smem, smem],
        out_specs=vmem,
        scratch_shapes=[
            pltpu.VMEM((D, 3 * WIDTH), bf16),
            pltpu.VMEM((4, ROWS, D), bf16),
            pltpu.VMEM((RUN, WIDTH), bf16),
            pltpu.VMEM((3 * RUN, 2 * WIDTH), bf16),
            pltpu.VMEM((3 * RUN, 128), bf16),
            pltpu.VMEM((RUN, 128), bf16),
            pltpu.VMEM((6, RUN, 256), f32),
            pltpu.VMEM((6, RUN, 128), f32),
            pltpu.VMEM((RUN, WIDTH), bf16),
            pltpu.VMEM((ROWS, D), bf16),
            pltpu.VMEM((4, PIECE, 2 * WIDTH), bf16),
            pltpu.VMEM((4, PIECE, 2 * WIDTH), bf16),
            pltpu.VMEM((4, WIDTH, D), bf16),
            dma((3,)), dma((3,)), dma((3,)),
            dma((4,)), dma((4,)), dma((4,)),
            dma((4,)), dma((4,)), dma((4,)), dma((4,)),
            dma((4, 4)), dma((4,)), dma((4, 4)), dma((4,)),
            dma((4,)), dma((4, 4)), dma((4,)), dma((4, 4)),
            dma((3, 3)), dma((3, 3)),
            dma, dma((3,)), dma((3,)), dma((3,)), dma((3,)), dma((3,)), dma((3,)), dma, dma,
        ],
        compiler_params=pltpu.CompilerParams(
            collective_id=0, has_side_effects=True, vmem_limit_bytes=63 * 2**20
        ),
        cost_estimate=pl.CostEstimate(flops=60_000_000_000, bytes_accessed=8_000_000, transcendentals=8_000_000),
        name="attend",
    )(frames, gain, w_query, w_key, w_value, w_out, band, lengths)


def local(frames, norm_gain, w_query, w_key, w_value, w_out, group_band, lengths):
    update = exchange_and_attend(
        frames[0], norm_gain[None], w_query, w_key, w_value, group_band[0], lengths, w_out
    )
    return update[None]


def solution(mesh):
    return jax.shard_map(
        local,
        mesh=mesh,
        in_specs=(
            P("dp", ("seq", "head"), None),
            P(),
            P("dp", "head"),
            P("dp", "head"),
            P("dp", "head"),
            P("head", "dp"),
            P("dp", "seq", None),
            P("dp"),
        ),
        out_specs=P("dp", ("seq", "head"), None),
        check_vma=False,
    )
```

```python
import functools

import jax
import jax.numpy as jnp
from jax import lax
from jax.experimental import pallas as pl
from jax.experimental.pallas import tpu as pltpu
from jax.sharding import PartitionSpec as P

MESH = pl.DeviceIdType.MESH
HD = 64
GROUP = 128
ROWS = 192
RUN = 768
WIDTH = 384
D = 1536
REACH = 6
PIECE = 48
QB = 256
FORBIDDEN = -1e30
epsilon = 1e-05


def kernel(
    frames, gain, w_query, w_key, w_value, w_out, marks, out,
    weights, normalized, other_marks, query, kv, bias, onehot, acc, top, context, gathered, relay_up, relay_down, landed_up, landed_down, projection,
    marks_send, marks_recv, w_send, w_recv, w_local, far_w_send, far_w_recv, line_w_send, line_w_recv, plane_w_send, plane_w_recv,
    on_send, out_send, block_recv, core_send, core_recv,
    up_send, up_recv, down_send, down_recv,
    spread_up_send, spread_up_recv, spread_down_send, spread_down_recv,
    far_up_send, far_up_recv, far_down_send, far_down_recv,
    last_up_send, last_up_recv, last_down_send, last_down_recv,
    ctx_send, ctx_recv,
    out_local, out_z_send, out_z_recv, out_x_send, out_x_recv, out_y_send, out_y_recv, out_core_send, out_core_recv,
):
    dp, seq, head = lax.axis_index("dp"), lax.axis_index("seq"), lax.axis_index("head")
    row, x = seq // 4, seq % 4
    y = seq // 16
    utterance = head // 2
    near = 1 - (dp + utterance) % 2
    is_near = near == 1
    group_of_heads = (head + 2 * (1 - near)) % 4
    other_core = (1 - dp, seq, head)
    place_on_line = head + dp * (3 - 2 * head)
    first_seq = row * 4
    has_up, has_down = row < 15, row > 0

    def copy(src, dst, send, recv, to):
        return pltpu.make_async_remote_copy(
            src_ref=src, dst_ref=dst, send_sem=send, recv_sem=recv, device_id=to, device_id_type=MESH
        )

    barrier = pltpu.get_barrier_semaphore()

    def greet(to):
        pl.semaphore_signal(barrier, inc=1, device_id=to, device_id_type=MESH)

    greet(other_core)
    for k in (1, 2, 3):
        greet((dp, seq, (head + k) % 4))
        greet((1 - dp, seq, (head + k) % 4))
        greet((dp, first_seq + (x + k) % 4, head))
        greet((dp, (seq + 16 * k) % 64, head))

    pl.when(has_up)(lambda: greet((dp, (seq + 4) % 64, head)))
    pl.when(has_down)(lambda: greet((dp, (seq + 60) % 64, head)))
    pl.semaphore_wait(barrier, 13 + (1 - (row + 1) // 16) + (row + 15) // 16)

    def swap_marks():
        return copy(marks, other_marks, marks_send, marks_recv, other_core)

    swap_marks().start()

    half = pl.ds(pl.multiple_of(dp * (D // 2), D // 2), D // 2)

    def weight_there(i, ref):
        part = weights.at[half, pl.ds(i * WIDTH, WIDTH)]
        return copy(ref, part, w_send.at[i], w_recv.at[i], other_core)

    def weight_here(i, ref):
        return pltpu.make_async_copy(ref, weights.at[half, pl.ds(i * WIDTH, WIDTH)], w_local.at[i])

    first, second = (1 - dp) * y + dp * x, (1 - dp) * x + dp * y

    def weight_far(i, ref):
        start = first * ROWS + second * PIECE
        return copy(
            ref.at[pl.ds(pl.multiple_of(start, 16), PIECE), :],
            weights.at[pl.ds(pl.multiple_of(dp * (D // 2) + start, 16), PIECE), pl.ds(i * WIDTH, WIDTH)],
            far_w_send.at[i], far_w_recv.at[dp, i], (utterance, seq, (head + 2) % 4),
        )

    def weight_arrived(core, i, ref):
        return copy(
            ref.at[pl.ds(0, PIECE), :], weights.at[pl.ds(0, PIECE), pl.ds(i * WIDTH, WIDTH)],
            far_w_send.at[i], far_w_recv.at[core, i], other_core,
        )

    def over_x(k):
        return (dp, first_seq + (x + k) % 4, head)

    def over_y(k):
        return (dp, (seq + 16 * k) % 64, head)

    def weight_line(core, k):
        start = core * (D // 2) + (x * ROWS + y * PIECE if core else y * ROWS + x * PIECE)
        part = weights.at[pl.ds(pl.multiple_of(start, 16), PIECE), :]
        return copy(
            part, part, line_w_send.at[core, k - 1], line_w_recv.at[core, k - 1], over_y(k) if core else over_x(k)
        )

    def weight_plane(core, k):
        start = core * (D // 2) + (x if core else y) * ROWS
        part = weights.at[pl.ds(pl.multiple_of(start, 16), ROWS), :]
        return copy(
            part, part, plane_w_send.at[core, k - 1], plane_w_recv.at[core, k - 1], over_x(k) if core else over_y(k)
        )

    for i, ref in enumerate((w_query, w_key, w_value)):
        weight_far(i, ref).start()

        @pl.when(is_near)
        def _():
            weight_here(i, ref).start()

        @pl.when(jnp.logical_not(is_near))
        def _():
            weight_there(i, ref).start()

    piece_rows = pl.ds(pl.multiple_of(y * 96 + x % 2 * 48, 16), 48)
    strip_rows = pl.ds(pl.multiple_of(y * 96, 16), 96)
    piece_from = pl.ds(pl.multiple_of(x // 2 * WIDTH, 128), WIDTH)
    piece_columns = pl.ds(pl.multiple_of(dp * (D // 2) + x // 2 * WIDTH, 128), WIDTH)

    def out_here():
        return pltpu.make_async_copy(
            w_out.at[piece_rows, piece_from], projection.at[head, piece_rows, piece_columns], out_local
        )

    def out_z(k):
        return copy(
            w_out.at[piece_rows, piece_from], projection.at[head, piece_rows, piece_columns],
            out_z_send.at[k - 1], out_z_recv.at[k - 1], (dp, seq, (head + k) % 4),
        )

    def out_x(k):
        part = projection.at[:, piece_rows, piece_columns]
        return copy(part, part, out_x_send.at[k - 1], out_x_recv.at[k - 1], (dp, first_seq + (x + k) % 4, head))

    def out_y(k):
        part = projection.at[:, strip_rows, half]
        return copy(part, part, out_y_send.at[k - 1], out_y_recv.at[k - 1], (dp, (seq + 16 * k) % 64, head))

    def out_core():
        part = projection.at[:, :, half]
        return copy(part, part, out_core_send, out_core_recv, (1 - dp, seq, head))

    out_here().start()
    for k in (2, 1, 3):
        out_z(k).start()

    values = frames[...].astype(jnp.float32)
    center = values - jnp.mean(values, axis=-1, keepdims=True)
    spread = jnp.mean(center * center, axis=-1, keepdims=True)
    normalized[head] = (center * lax.rsqrt(spread + epsilon) * gain[...][None, :]).astype(jnp.bfloat16)

    step = 1 - 2 * dp
    onward = (dp, seq, (head + 4 - step) % 4)
    back = (dp, seq, (head + 4 + step) % 4)

    def to_onward(b):
        return copy(normalized.at[b], normalized.at[b], on_send.at[b], block_recv.at[b], onward)

    def to_back():
        return copy(normalized.at[head], normalized.at[head], out_send, block_recv.at[head], back)

    def to_core(b):
        return copy(normalized.at[b], normalized.at[4 + b], core_send.at[b], core_recv.at[b], other_core)

    pl.when(place_on_line > 0)(lambda: to_onward(head).start())
    pl.when(place_on_line == 0)(lambda: to_back().start())

    onehot[...] = (
        lax.broadcasted_iota(jnp.int32, (RUN, 128), 0) // GROUP
        == lax.broadcasted_iota(jnp.int32, (RUN, 128), 1)
    ).astype(jnp.bfloat16)
    swap_marks().wait_recv()
    seen_marks = marks[...] * near + other_marks[...] * (1 - near)
    length = seen_marks[12:13, :]
    lane = lax.broadcasted_iota(jnp.int32, (1, 128), 1)
    within = lax.broadcasted_iota(jnp.int32, (GROUP, 128), 0)
    for kg in range(3 * REACH):
        seen = jnp.zeros((1, 128), jnp.int32)
        own = jnp.zeros((1, 128), jnp.int32)
        for g in range(REACH):
            offset = kg - REACH - g
            if offset == 0:
                own = jnp.where(lane == g, 1, own)
            elif abs(offset) <= REACH:
                column = offset + REACH if offset < 0 else offset + REACH - 1
                seen = jnp.where(lane == g, seen_marks[column:column + 1, :], seen)
        group = seq * REACH - REACH + kg
        inside = jnp.where((group >= 0) & (group < 64 * REACH), 1, 0)
        alive = (group * GROUP + within < length).astype(jnp.int32) * inside
        allowed = (jnp.where(seen == 1, 1, 0) * alive + own) > 0
        bias[kg * GROUP:(kg + 1) * GROUP, :] = jnp.where(allowed, 0.0, FORBIDDEN).astype(jnp.bfloat16)

    @pl.when(seq == 0)
    def _():
        kv[0:RUN, :] = jnp.zeros((RUN, 2 * WIDTH), jnp.bfloat16)

    @pl.when(seq == 63)
    def _():
        kv[2 * RUN:3 * RUN, :] = jnp.zeros((RUN, 2 * WIDTH), jnp.bfloat16)

    def spread_out_weights():
        out_here().wait()
        for k in (1, 2, 3):
            out_z(k).wait_recv()
        for k in (2, 1, 3):
            out_x(k).start()

    @pl.when(is_near)
    def _():
        for i, ref in enumerate((w_query, w_key, w_value)):
            weight_here(i, ref).wait()
            weight_there(i, ref).wait_recv()
        spread_out_weights()

    @pl.when(jnp.logical_not(is_near))
    def _():
        for core in range(2):
            for i, ref in enumerate((w_query, w_key, w_value)):
                weight_arrived(core, i, ref).wait_recv()
            for k in (2, 1, 3):
                weight_line(core, k).start()
        spread_out_weights()
        for core in range(2):
            for k in (1, 2, 3):
                weight_line(core, k).wait_recv()
            for k in (2, 1, 3):
                weight_plane(core, k).start()

        @pl.when(place_on_line == 2)
        def _():
            to_onward(3 * utterance).wait_recv()
            to_onward(3 * utterance).start()

        for k in (1, 2, 3):
            out_x(k).wait_recv()
        for k in (2, 1, 3):
            out_y(k).start()
        for core in range(2):
            for k in (1, 2, 3):
                weight_plane(core, k).wait_recv()

    def place(side, b, q=None):
        start, size = side * RUN + b * ROWS, ROWS
        if q is not None:
            start, size = start + q * PIECE, PIECE
        return kv.at[pl.ds(pl.multiple_of(start, 16), size), :]

    def up_near(b):
        return copy(place(1, b), place(0, b), up_send.at[b], up_recv.at[b], (dp, (seq + 1) % 64, head))

    def down_near(b):
        return copy(place(1, b), place(2, b), down_send.at[b], down_recv.at[b], (dp, (seq + 63) % 64, head))

    def up_spread(b, q):
        return copy(
            place(1, b, q), relay_up.at[b], spread_up_send.at[b, q], spread_up_recv.at[b], (dp, first_seq + q, head)
        )

    def down_spread(b, q):
        return copy(
            place(1, b, q), relay_down.at[b], spread_down_send.at[b, q], spread_down_recv.at[b],
            (dp, first_seq + q, head),
        )

    def up_far(b, src, dst):
        return copy(src, dst, far_up_send.at[b], far_up_recv.at[b], (dp, (seq + 4) % 64, head))

    def down_far(b, src, dst):
        return copy(src, dst, far_down_send.at[b], far_down_recv.at[b], (dp, (seq + 60) % 64, head))

    def up_last(b, q):
        return copy(
            landed_up.at[b], place(0, b, q), last_up_send.at[b], last_up_recv.at[b, q], (dp, first_seq, head)
        )

    def down_last(b, q):
        return copy(
            landed_down.at[b], place(2, b, q), last_down_send.at[b], last_down_recv.at[b, q],
            (dp, first_seq + 3, head),
        )

    def send_near(b):
        pl.when(x < 3)(lambda: up_near(b).start())
        pl.when(x > 0)(lambda: down_near(b).start())

    def send_block(b):
        @pl.when((x == 3) & has_up)
        def _():
            for q in range(3):
                up_spread(b, q).start()

        @pl.when((x == 0) & has_down)
        def _():
            for q in range(1, 4):
                down_spread(b, q).start()

    def relay_block(b):
        @pl.when(has_up)
        def _():
            pl.when(x < 3)(lambda: up_spread(b, x).wait_recv())
            pl.when(x == 0)(lambda: up_far(b, relay_up.at[b], place(0, b, 0)).start())
            pl.when((x > 0) & (x < 3))(lambda: up_far(b, relay_up.at[b], landed_up.at[b]).start())
            pl.when(x == 3)(lambda: up_far(b, place(1, b, 3), landed_up.at[b]).start())

        @pl.when(has_down)
        def _():
            pl.when(x > 0)(lambda: down_spread(b, x).wait_recv())
            pl.when(x == 3)(lambda: down_far(b, relay_down.at[b], place(2, b, 3)).start())
            pl.when((x > 0) & (x < 3))(lambda: down_far(b, relay_down.at[b], landed_down.at[b]).start())
            pl.when(x == 0)(lambda: down_far(b, place(1, b, 0), landed_down.at[b]).start())

    def deliver_block(b):
        @pl.when((x > 0) & has_down)
        def _():
            up_far(b, relay_up.at[b], landed_up.at[b]).wait_recv()
            up_last(b, x).start()

        @pl.when((x < 3) & has_up)
        def _():
            down_far(b, relay_down.at[b], landed_down.at[b]).wait_recv()
            down_last(b, x).start()

    far_end = head // 2
    mirrored = head + far_end * (3 - 2 * head)

    def nth(t):
        near = t // 2 * 2 + (t + mirrored * (1 - t // 2)) % 2
        return near + far_end * (3 - 2 * near)

    def project(t, carry):
        b = nth(t)

        @pl.when(is_near)
        def _():
            pl.when(t > 0)(lambda: to_onward(b).wait_recv())
            pl.when((place_on_line == 1) & (t > 1))(lambda: to_onward(b).start())
            to_core(b).start()

        @pl.when(jnp.logical_not(is_near))
        def _():
            to_core(b).wait_recv()

        @pl.when(is_near & (t == 2))
        def _():
            for k in (1, 2, 3):
                out_x(k).wait_recv()
            for k in (2, 1, 3):
                out_y(k).start()

        rows = normalized[b + 4 * (1 - near)]
        product = jnp.dot(rows, weights[...], preferred_element_type=jnp.float32).astype(jnp.bfloat16)
        start = pl.multiple_of(b * ROWS, ROWS)
        query[pl.ds(start, ROWS), :] = product[:, :WIDTH] * jnp.bfloat16(0.125)
        kv[pl.ds(pl.multiple_of(RUN + start, ROWS), ROWS), :] = product[:, WIDTH:]
        send_block(b)
        pl.when(is_near)(lambda: send_near(b))
        return carry

    lax.fori_loop(0, 4, project, 0)

    def relay(t, carry):
        relay_block(nth(t))
        return carry

    lax.fori_loop(0, 4, relay, 0)

    @pl.when(jnp.logical_not(is_near))
    def _():
        for t in range(4):
            send_near(nth(t))

    low_half = lax.broadcasted_iota(jnp.int32, (QB, 128), 1) < HD

    def attend(p, query_start, key_start, keys, first):
        lanes = pl.ds(pl.multiple_of(p * 128, 128), 128)
        value_lanes = pl.ds(pl.multiple_of(WIDTH + p * 128, 128), 128)
        key_rows = pl.ds(pl.multiple_of(key_start, QB), keys)
        query_rows = pl.ds(pl.multiple_of(query_start, QB), QB)
        key_tile = jnp.concatenate([kv[key_rows, lanes], bias[key_rows, :]], axis=1)
        value_tile = jnp.concatenate([kv[key_rows, value_lanes], jnp.ones((keys, 128), jnp.bfloat16)], axis=1)
        query_tile = query[query_rows, lanes]
        marks = onehot[query_rows, :]
        for hh in range(2):
            h = p * 2 + hh
            mine = jnp.where(low_half == (hh == 0), query_tile, jnp.zeros_like(query_tile))
            scores = lax.dot_general(
                jnp.concatenate([mine, marks], axis=1), key_tile, (((1,), (1,)), ((), ())),
                preferred_element_type=jnp.float32,
            )
            here = jnp.max(scores, axis=-1, keepdims=True)
            if first:
                best = here
            else:
                before = top[h, query_rows, :][:, :1]
                best = jnp.maximum(before, here)
            rounded = jnp.exp(scores - best).astype(jnp.bfloat16)
            part = jnp.dot(rounded, value_tile, preferred_element_type=jnp.float32)
            if not first:
                part = part + acc[h, query_rows, :] * jnp.exp(before - best)
            acc[h, query_rows, :] = part
            top[h, query_rows, :] = jnp.broadcast_to(best, (QB, 128))

    def own_part(p, carry):
        for j in range(3):
            attend(p, j * QB, RUN, RUN, True)

        @pl.when(p == 0)
        def _():
            deliver_block(nth(0))
            deliver_block(nth(1))

        pl.when(p > 0)(lambda: deliver_block(nth(p + 1)))
        return carry

    lax.fori_loop(0, 3, own_part, 0)

    def wait_side(side):
        @pl.when(side == 0)
        def _():
            @pl.when(x > 0)
            def _():
                for b in range(4):
                    up_near(b).wait_recv()

            @pl.when((x == 0) & has_down)
            def _():
                for b in range(4):
                    up_far(b, relay_up.at[b], place(0, b, 0)).wait_recv()
                    for q in range(1, 4):
                        up_last(b, q).wait_recv()

        @pl.when(side == 1)
        def _():
            @pl.when(x < 3)
            def _():
                for b in range(4):
                    down_near(b).wait_recv()

            @pl.when((x == 3) & has_up)
            def _():
                for b in range(4):
                    down_far(b, relay_down.at[b], place(2, b, 3)).wait_recv()
                    for q in range(3):
                        down_last(b, q).wait_recv()

    def side_part(p, side):
        for j in range(3):
            query_start = j * QB + side * (2 * QB - 2 * j * QB)
            key_start = j * QB + side * (2 * RUN - j * QB)
            attend(p, query_start, key_start, RUN - j * QB, False)

    first_side = 1 - (x + 3) // 4
    wait_side(first_side)

    def early_part(p, carry):
        side_part(p, first_side)
        return carry

    lax.fori_loop(0, 3, early_part, 0)
    for k in (1, 2, 3):
        out_y(k).wait_recv()
    out_core().start()
    last_side = 1 - first_side
    wait_side(last_side)

    def ctx_copy(p, to, heads):
        return copy(
            context.at[pl.ds(to * ROWS, ROWS), pl.ds(pl.multiple_of(p * 128, 128), 128)],
            gathered.at[:, pl.ds(pl.multiple_of(heads * WIDTH + p * 128, 128), 128)],
            ctx_send.at[p, to], ctx_recv.at[p, heads], (utterance, seq, to),
        )

    def keeps(to):
        return is_near & (head == to)

    def late_part(p, carry):
        side_part(p, last_side)
        lanes = pl.ds(pl.multiple_of(p * 128, 128), 128)
        for j in range(3):
            rows = pl.ds(j * QB, QB)
            low, high = acc[p * 2, rows, :], acc[p * 2 + 1, rows, :]
            context[rows, lanes] = jnp.where(
                low_half, low[:, :128] / low[:, 128:], high[:, :128] / high[:, 128:]
            ).astype(jnp.bfloat16)
        for to in range(4):
            pl.when(jnp.logical_not(keeps(to)))(lambda: ctx_copy(p, to, group_of_heads).start())
        return carry

    lax.fori_loop(0, 3, late_part, 0)

    @pl.when(is_near)
    def _():
        own_lanes = pl.ds(pl.multiple_of(head * WIDTH, 128), WIDTH)
        gathered[:, own_lanes] = context[pl.ds(pl.multiple_of(head * ROWS, ROWS), ROWS), :]

    swap_marks().wait_send()
    for i, ref in enumerate((w_query, w_key, w_value)):
        weight_far(i, ref).wait_send()

    @pl.when(jnp.logical_not(is_near))
    def _():
        for i, ref in enumerate((w_query, w_key, w_value)):
            weight_there(i, ref).wait_send()
        for core in range(2):
            for k in (1, 2, 3):
                weight_line(core, k).wait_send()
                weight_plane(core, k).wait_send()

    pl.when(place_on_line > 0)(lambda: to_onward(head).wait_send())
    pl.when(place_on_line == 0)(lambda: to_back().wait_send())
    pl.when(place_on_line == 2)(lambda: to_onward(3 * utterance).wait_send())

    @pl.when(place_on_line == 1)
    def _():
        for t in (2, 3):
            to_onward(nth(t)).wait_send()

    for b in range(4):
        pl.when(is_near)(lambda: to_core(b).wait_send())
        pl.when(x < 3)(lambda: up_near(b).wait_send())
        pl.when(x > 0)(lambda: down_near(b).wait_send())

        @pl.when((x == 3) & has_up)
        def _():
            for q in range(3):
                up_spread(b, q).wait_send()

        @pl.when((x == 0) & has_down)
        def _():
            for q in range(1, 4):
                down_spread(b, q).wait_send()

        pl.when(has_up)(lambda: up_far(b, relay_up.at[b], landed_up.at[b]).wait_send())
        pl.when(has_down)(lambda: down_far(b, relay_down.at[b], landed_down.at[b]).wait_send())
        pl.when((x > 0) & has_down)(lambda: up_last(b, x).wait_send())
        pl.when((x < 3) & has_up)(lambda: down_last(b, x).wait_send())
    for k in (1, 2, 3):
        out_z(k).wait_send()
        out_x(k).wait_send()
        out_y(k).wait_send()
    out_core().wait()
    for g in range(4):
        for p in range(3):
            pl.when(jnp.logical_not(keeps(g)))(lambda: ctx_copy(p, g, group_of_heads).wait_send())
            pl.when(jnp.logical_not(keeps(g)))(lambda: ctx_copy(p, g, g).wait_recv())
    total = jnp.dot(gathered[:, :WIDTH], projection[0], preferred_element_type=jnp.float32)
    for g in range(1, 4):
        total += jnp.dot(
            gathered[:, g * WIDTH:(g + 1) * WIDTH], projection[g], preferred_element_type=jnp.float32
        )
    out[...] = total.astype(jnp.bfloat16)


def exchange_and_attend(frames, gain, w_query, w_key, w_value, w_out, marks):
    vmem, anywhere = (pl.BlockSpec(memory_space=m) for m in (pltpu.VMEM, pl.ANY))
    dma = pltpu.SemaphoreType.DMA
    bf16, f32 = jnp.bfloat16, jnp.float32
    return pl.pallas_call(
        kernel,
        out_shape=jax.ShapeDtypeStruct((ROWS, D), bf16),
        in_specs=[vmem, vmem, anywhere, anywhere, anywhere, anywhere, vmem],
        out_specs=vmem,
        scratch_shapes=[
            pltpu.VMEM((D, 3 * WIDTH), bf16),
            pltpu.VMEM((8, ROWS, D), bf16),
            pltpu.VMEM((16, 128), jnp.int32),
            pltpu.VMEM((RUN, WIDTH), bf16),
            pltpu.VMEM((3 * RUN, 2 * WIDTH), bf16),
            pltpu.VMEM((3 * RUN, 128), bf16),
            pltpu.VMEM((RUN, 128), bf16),
            pltpu.VMEM((6, RUN, 256), f32),
            pltpu.VMEM((6, RUN, 128), f32),
            pltpu.VMEM((RUN, WIDTH), bf16),
            pltpu.VMEM((ROWS, D), bf16),
            pltpu.VMEM((4, PIECE, 2 * WIDTH), bf16),
            pltpu.VMEM((4, PIECE, 2 * WIDTH), bf16),
            pltpu.VMEM((4, PIECE, 2 * WIDTH), bf16),
            pltpu.VMEM((4, PIECE, 2 * WIDTH), bf16),
            pltpu.VMEM((4, WIDTH, D), bf16),
            dma, dma, dma((3,)), dma((3,)), dma((3,)),
            dma((3,)), dma((2, 3)), dma((2, 3)), dma((2, 3)), dma((2, 3)), dma((2, 3)),
            dma((4,)), dma, dma((4,)), dma((4,)), dma((4,)),
            dma((4,)), dma((4,)), dma((4,)), dma((4,)),
            dma((4, 4)), dma((4,)), dma((4, 4)), dma((4,)),
            dma((4,)), dma((4,)), dma((4,)), dma((4,)),
            dma((4,)), dma((4, 4)), dma((4,)), dma((4, 4)),
            dma((3, 4)), dma((3, 4)),
            dma, dma((3,)), dma((3,)), dma((3,)), dma((3,)), dma((3,)), dma((3,)), dma, dma,
        ],
        compiler_params=pltpu.CompilerParams(
            collective_id=0, has_side_effects=True, vmem_limit_bytes=63 * 2**20
        ),
        cost_estimate=pl.CostEstimate(flops=60_000_000_000, bytes_accessed=8_000_000, transcendentals=8_000_000),
        name="attend",
    )(frames, gain, w_query, w_key, w_value, w_out, marks)


def local(frames, norm_gain, w_query, w_key, w_value, w_out, group_band, lengths):
    band = jnp.pad(group_band[0].T, ((0, 4), (0, 128 - REACH)))
    marks = jnp.where(lax.broadcasted_iota(jnp.int32, (16, 128), 0) == 12, lengths[0], band)
    update = exchange_and_attend(frames[0], norm_gain, w_query, w_key, w_value, w_out, marks)
    return update[None]


def solution(mesh):
    return jax.shard_map(
        local,
        mesh=mesh,
        in_specs=(
            P("dp", ("seq", "head"), None),
            P(),
            P("dp", "head"),
            P("dp", "head"),
            P("dp", "head"),
            P("head", "dp"),
            P("dp", "seq", None),
            P("dp"),
        ),
        out_specs=P("dp", ("seq", "head"), None),
        check_vma=False,
    )
```

```python
import functools

import jax
import jax.numpy as jnp
from jax import lax
from jax.experimental import pallas as pl
from jax.experimental.pallas import tpu as pltpu
from jax.sharding import PartitionSpec as P

MESH = pl.DeviceIdType.MESH
HD = 64
GROUP = 128
ROWS = 192
RUN = 768
WIDTH = 384
D = 1536
REACH = 6
PIECE = 48
QB = 256
FORBIDDEN = -1e30
epsilon = 1e-05


def kernel(
    frames, gain, w_query, w_key, w_value, w_out, marks, out,
    weights, normalized, other_marks, query, kv, bias, onehot, acc, top, context, gathered, relay_up, relay_down, landed_up, landed_down, projection,
    marks_send, marks_recv, w_send, w_recv, w_local, far_w_send, far_w_recv, line_w_send, line_w_recv, plane_w_send, plane_w_recv,
    on_send, out_send, block_recv, core_send, core_recv,
    up_send, up_recv, down_send, down_recv,
    spread_up_send, spread_up_recv, spread_down_send, spread_down_recv,
    far_up_send, far_up_recv, far_down_send, far_down_recv,
    last_up_send, last_up_recv, last_down_send, last_down_recv,
    ctx_send, ctx_recv,
    out_local, out_z_send, out_z_recv, out_x_send, out_x_recv, out_y_send, out_y_recv, out_core_send, out_core_recv,
):
    dp, seq, head = lax.axis_index("dp"), lax.axis_index("seq"), lax.axis_index("head")
    row, x = seq // 4, seq % 4
    y = seq // 16
    utterance = head // 2
    near = 1 - (dp + utterance) % 2
    is_near = near == 1
    group_of_heads = (head + 2 * (1 - near)) % 4
    other_core = (1 - dp, seq, head)
    place_on_line = head + dp * (3 - 2 * head)
    first_seq = row * 4
    has_up, has_down = row < 15, row > 0

    def copy(src, dst, send, recv, to):
        return pltpu.make_async_remote_copy(
            src_ref=src, dst_ref=dst, send_sem=send, recv_sem=recv, device_id=to, device_id_type=MESH
        )

    barrier = pltpu.get_barrier_semaphore()

    def greet(to):
        pl.semaphore_signal(barrier, inc=1, device_id=to, device_id_type=MESH)

    greet(other_core)
    for k in (1, 2, 3):
        greet((dp, seq, (head + k) % 4))
        greet((1 - dp, seq, (head + k) % 4))
        greet((dp, first_seq + (x + k) % 4, head))
        greet((dp, (seq + 16 * k) % 64, head))

    pl.when(has_up)(lambda: greet((dp, (seq + 4) % 64, head)))
    pl.when(has_down)(lambda: greet((dp, (seq + 60) % 64, head)))
    pl.semaphore_wait(barrier, 13 + (1 - (row + 1) // 16) + (row + 15) // 16)

    def swap_marks():
        return copy(marks, other_marks, marks_send, marks_recv, other_core)

    swap_marks().start()

    half = pl.ds(pl.multiple_of(dp * (D // 2), D // 2), D // 2)

    def weight_there(i, ref):
        part = weights.at[half, pl.ds(i * WIDTH, WIDTH)]
        return copy(ref, part, w_send.at[i], w_recv.at[i], other_core)

    def weight_here(i, ref):
        return pltpu.make_async_copy(ref, weights.at[half, pl.ds(i * WIDTH, WIDTH)], w_local.at[i])

    first, second = (1 - dp) * y + dp * x, (1 - dp) * x + dp * y

    def weight_far(i, ref):
        start = first * ROWS + second * PIECE
        return copy(
            ref.at[pl.ds(pl.multiple_of(start, 16), PIECE), :],
            weights.at[pl.ds(pl.multiple_of(dp * (D // 2) + start, 16), PIECE), pl.ds(i * WIDTH, WIDTH)],
            far_w_send.at[i], far_w_recv.at[dp, i], (utterance, seq, (head + 2) % 4),
        )

    def weight_arrived(core, i, ref):
        return copy(
            ref.at[pl.ds(0, PIECE), :], weights.at[pl.ds(0, PIECE), pl.ds(i * WIDTH, WIDTH)],
            far_w_send.at[i], far_w_recv.at[core, i], other_core,
        )

    def over_x(k):
        return (dp, first_seq + (x + k) % 4, head)

    def over_y(k):
        return (dp, (seq + 16 * k) % 64, head)

    def weight_line(core, k):
        start = core * (D // 2) + (x * ROWS + y * PIECE if core else y * ROWS + x * PIECE)
        part = weights.at[pl.ds(pl.multiple_of(start, 16), PIECE), :]
        return copy(
            part, part, line_w_send.at[core, k - 1], line_w_recv.at[core, k - 1], over_y(k) if core else over_x(k)
        )

    def weight_plane(core, k):
        start = core * (D // 2) + (x if core else y) * ROWS
        part = weights.at[pl.ds(pl.multiple_of(start, 16), ROWS), :]
        return copy(
            part, part, plane_w_send.at[core, k - 1], plane_w_recv.at[core, k - 1], over_x(k) if core else over_y(k)
        )

    for i, ref in enumerate((w_query, w_key, w_value)):
        weight_far(i, ref).start()

        @pl.when(is_near)
        def _():
            weight_here(i, ref).start()

        @pl.when(jnp.logical_not(is_near))
        def _():
            weight_there(i, ref).start()

    piece_rows = pl.ds(pl.multiple_of(y * 96 + x % 2 * 48, 16), 48)
    strip_rows = pl.ds(pl.multiple_of(y * 96, 16), 96)
    piece_from = pl.ds(pl.multiple_of(x // 2 * WIDTH, 128), WIDTH)
    piece_columns = pl.ds(pl.multiple_of(dp * (D // 2) + x // 2 * WIDTH, 128), WIDTH)

    def out_here():
        return pltpu.make_async_copy(
            w_out.at[piece_rows, piece_from], projection.at[head, piece_rows, piece_columns], out_local
        )

    def out_z(k):
        return copy(
            w_out.at[piece_rows, piece_from], projection.at[head, piece_rows, piece_columns],
            out_z_send.at[k - 1], out_z_recv.at[k - 1], (dp, seq, (head + k) % 4),
        )

    def out_x(k):
        part = projection.at[:, piece_rows, piece_columns]
        return copy(part, part, out_x_send.at[k - 1], out_x_recv.at[k - 1], (dp, first_seq + (x + k) % 4, head))

    def out_y(k):
        part = projection.at[:, strip_rows, half]
        return copy(part, part, out_y_send.at[k - 1], out_y_recv.at[k - 1], (dp, (seq + 16 * k) % 64, head))

    def out_core():
        part = projection.at[:, :, half]
        return copy(part, part, out_core_send, out_core_recv, (1 - dp, seq, head))

    out_here().start()
    for k in (2, 1, 3):
        out_z(k).start()

    values = frames[...].astype(jnp.float32)
    center = values - jnp.mean(values, axis=-1, keepdims=True)
    spread = jnp.mean(center * center, axis=-1, keepdims=True)
    normalized[head] = (center * lax.rsqrt(spread + epsilon) * gain[...][None, :]).astype(jnp.bfloat16)

    step = 1 - 2 * dp
    onward = (dp, seq, (head + 4 - step) % 4)
    back = (dp, seq, (head + 4 + step) % 4)

    def to_onward(b):
        return copy(normalized.at[b], normalized.at[b], on_send.at[b], block_recv.at[b], onward)

    def to_back():
        return copy(normalized.at[head], normalized.at[head], out_send, block_recv.at[head], back)

    def to_core(b):
        return copy(normalized.at[b], normalized.at[4 + b], core_send.at[b], core_recv.at[b], other_core)

    pl.when(place_on_line > 0)(lambda: to_onward(head).start())
    pl.when(place_on_line == 0)(lambda: to_back().start())

    onehot[...] = (
        lax.broadcasted_iota(jnp.int32, (RUN, 128), 0) // GROUP
        == lax.broadcasted_iota(jnp.int32, (RUN, 128), 1)
    ).astype(jnp.bfloat16)
    swap_marks().wait_recv()
    seen_marks = marks[...] * near + other_marks[...] * (1 - near)
    length = seen_marks[12:13, :]
    lane = lax.broadcasted_iota(jnp.int32, (1, 128), 1)
    within = lax.broadcasted_iota(jnp.int32, (GROUP, 128), 0)
    for kg in range(3 * REACH):
        seen = jnp.zeros((1, 128), jnp.int32)
        own = jnp.zeros((1, 128), jnp.int32)
        for g in range(REACH):
            offset = kg - REACH - g
            if offset == 0:
                own = jnp.where(lane == g, 1, own)
            elif abs(offset) <= REACH:
                column = offset + REACH if offset < 0 else offset + REACH - 1
                seen = jnp.where(lane == g, seen_marks[column:column + 1, :], seen)
        group = seq * REACH - REACH + kg
        inside = jnp.where((group >= 0) & (group < 64 * REACH), 1, 0)
        alive = (group * GROUP + within < length).astype(jnp.int32) * inside
        allowed = (jnp.where(seen == 1, 1, 0) * alive + own) > 0
        bias[kg * GROUP:(kg + 1) * GROUP, :] = jnp.where(allowed, 0.0, FORBIDDEN).astype(jnp.bfloat16)

    @pl.when(seq == 0)
    def _():
        kv[0:RUN, :] = jnp.zeros((RUN, 2 * WIDTH), jnp.bfloat16)

    @pl.when(seq == 63)
    def _():
        kv[2 * RUN:3 * RUN, :] = jnp.zeros((RUN, 2 * WIDTH), jnp.bfloat16)

    def spread_out_weights():
        out_here().wait()
        for k in (1, 2, 3):
            out_z(k).wait_recv()
        for k in (2, 1, 3):
            out_x(k).start()

    @pl.when(is_near)
    def _():
        for i, ref in enumerate((w_query, w_key, w_value)):
            weight_here(i, ref).wait()
            weight_there(i, ref).wait_recv()
        spread_out_weights()

    @pl.when(jnp.logical_not(is_near))
    def _():
        for core in range(2):
            for i, ref in enumerate((w_query, w_key, w_value)):
                weight_arrived(core, i, ref).wait_recv()
            for k in (2, 1, 3):
                weight_line(core, k).start()
        spread_out_weights()
        for core in range(2):
            for k in (1, 2, 3):
                weight_line(core, k).wait_recv()
            for k in (2, 1, 3):
                weight_plane(core, k).start()

        @pl.when(place_on_line == 2)
        def _():
            to_onward(3 * utterance).wait_recv()
            to_onward(3 * utterance).start()

        for k in (1, 2, 3):
            out_x(k).wait_recv()
        for k in (2, 1, 3):
            out_y(k).start()
        for core in range(2):
            for k in (1, 2, 3):
                weight_plane(core, k).wait_recv()

    def place(side, b, q=None):
        start, size = side * RUN + b * ROWS, ROWS
        if q is not None:
            start, size = start + q * PIECE, PIECE
        return kv.at[pl.ds(pl.multiple_of(start, 16), size), :]

    def up_near(b):
        return copy(place(1, b), place(0, b), up_send.at[b], up_recv.at[b], (dp, (seq + 1) % 64, head))

    def down_near(b):
        return copy(place(1, b), place(2, b), down_send.at[b], down_recv.at[b], (dp, (seq + 63) % 64, head))

    def up_spread(b, q):
        return copy(
            place(1, b, q), relay_up.at[b], spread_up_send.at[b, q], spread_up_recv.at[b], (dp, first_seq + q, head)
        )

    def down_spread(b, q):
        return copy(
            place(1, b, q), relay_down.at[b], spread_down_send.at[b, q], spread_down_recv.at[b],
            (dp, first_seq + q, head),
        )

    def up_far(b, src, dst):
        return copy(src, dst, far_up_send.at[b], far_up_recv.at[b], (dp, (seq + 4) % 64, head))

    def down_far(b, src, dst):
        return copy(src, dst, far_down_send.at[b], far_down_recv.at[b], (dp, (seq + 60) % 64, head))

    def up_last(b, q):
        return copy(
            landed_up.at[b], place(0, b, q), last_up_send.at[b], last_up_recv.at[b, q], (dp, first_seq, head)
        )

    def down_last(b, q):
        return copy(
            landed_down.at[b], place(2, b, q), last_down_send.at[b], last_down_recv.at[b, q],
            (dp, first_seq + 3, head),
        )

    def send_near(b):
        pl.when(x < 3)(lambda: up_near(b).start())
        pl.when(x > 0)(lambda: down_near(b).start())

    def send_block(b):
        @pl.when((x == 3) & has_up)
        def _():
            for q in range(3):
                up_spread(b, q).start()

        @pl.when((x == 0) & has_down)
        def _():
            for q in range(1, 4):
                down_spread(b, q).start()

    def relay_block(b):
        @pl.when(has_up)
        def _():
            pl.when(x < 3)(lambda: up_spread(b, x).wait_recv())
            pl.when(x == 0)(lambda: up_far(b, relay_up.at[b], place(0, b, 0)).start())
            pl.when((x > 0) & (x < 3))(lambda: up_far(b, relay_up.at[b], landed_up.at[b]).start())
            pl.when(x == 3)(lambda: up_far(b, place(1, b, 3), landed_up.at[b]).start())

        @pl.when(has_down)
        def _():
            pl.when(x > 0)(lambda: down_spread(b, x).wait_recv())
            pl.when(x == 3)(lambda: down_far(b, relay_down.at[b], place(2, b, 3)).start())
            pl.when((x > 0) & (x < 3))(lambda: down_far(b, relay_down.at[b], landed_down.at[b]).start())
            pl.when(x == 0)(lambda: down_far(b, place(1, b, 0), landed_down.at[b]).start())

    def deliver_block(b):
        @pl.when((x > 0) & has_down)
        def _():
            up_far(b, relay_up.at[b], landed_up.at[b]).wait_recv()
            up_last(b, x).start()

        @pl.when((x < 3) & has_up)
        def _():
            down_far(b, relay_down.at[b], landed_down.at[b]).wait_recv()
            down_last(b, x).start()

    far_end = head // 2
    mirrored = head + far_end * (3 - 2 * head)

    def nth(t):
        near = t // 2 * 2 + (t + mirrored * (1 - t // 2)) % 2
        return near + far_end * (3 - 2 * near)

    def project(t, carry):
        b = nth(t)

        @pl.when(is_near)
        def _():
            pl.when(t > 0)(lambda: to_onward(b).wait_recv())
            pl.when((place_on_line == 1) & (t > 1))(lambda: to_onward(b).start())
            to_core(b).start()

        @pl.when(jnp.logical_not(is_near))
        def _():
            to_core(b).wait_recv()

        @pl.when(is_near & (t == 1))
        def _():
            for k in (1, 2, 3):
                out_x(k).wait_recv()
            for k in (2, 1, 3):
                out_y(k).start()

        rows = normalized[b + 4 * (1 - near)]
        product = jnp.dot(rows, weights[...], preferred_element_type=jnp.float32).astype(jnp.bfloat16)
        start = pl.multiple_of(b * ROWS, ROWS)
        query[pl.ds(start, ROWS), :] = product[:, :WIDTH] * jnp.bfloat16(0.125)
        kv[pl.ds(pl.multiple_of(RUN + start, ROWS), ROWS), :] = product[:, WIDTH:]
        send_block(b)
        pl.when(is_near)(lambda: send_near(b))
        return carry

    lax.fori_loop(0, 4, project, 0)

    def relay(t, carry):
        relay_block(nth(t))
        return carry

    @pl.when(jnp.logical_not(is_near))
    def _():
        for t in range(4):
            send_near(nth(t))

    lax.fori_loop(0, 4, relay, 0)

    low_half = lax.broadcasted_iota(jnp.int32, (QB, 128), 1) < HD

    def attend(p, query_start, key_start, keys, first):
        lanes = pl.ds(pl.multiple_of(p * 128, 128), 128)
        value_lanes = pl.ds(pl.multiple_of(WIDTH + p * 128, 128), 128)
        key_rows = pl.ds(pl.multiple_of(key_start, QB), keys)
        query_rows = pl.ds(pl.multiple_of(query_start, QB), QB)
        key_tile = jnp.concatenate([kv[key_rows, lanes], bias[key_rows, :]], axis=1)
        value_tile = jnp.concatenate([kv[key_rows, value_lanes], jnp.ones((keys, 128), jnp.bfloat16)], axis=1)
        query_tile = query[query_rows, lanes]
        marks = onehot[query_rows, :]
        for hh in range(2):
            h = p * 2 + hh
            mine = jnp.where(low_half == (hh == 0), query_tile, jnp.zeros_like(query_tile))
            scores = lax.dot_general(
                jnp.concatenate([mine, marks], axis=1), key_tile, (((1,), (1,)), ((), ())),
                preferred_element_type=jnp.float32,
            )
            here = jnp.max(scores, axis=-1, keepdims=True)
            if first:
                best = here
            else:
                before = top[h, query_rows, :][:, :1]
                best = jnp.maximum(before, here)
            rounded = jnp.exp(scores - best).astype(jnp.bfloat16)
            part = jnp.dot(rounded, value_tile, preferred_element_type=jnp.float32)
            if not first:
                part = part + acc[h, query_rows, :] * jnp.exp(before - best)
            acc[h, query_rows, :] = part
            top[h, query_rows, :] = jnp.broadcast_to(best, (QB, 128))

    def own_part(p, carry):
        for j in range(3):
            attend(p, j * QB, RUN, RUN, True)

        @pl.when(p == 0)
        def _():
            deliver_block(nth(0))
            deliver_block(nth(1))

        pl.when(p > 0)(lambda: deliver_block(nth(p + 1)))
        return carry

    lax.fori_loop(0, 3, own_part, 0)

    def wait_side(side):
        @pl.when(side == 0)
        def _():
            @pl.when(x > 0)
            def _():
                for b in range(4):
                    up_near(b).wait_recv()

            @pl.when((x == 0) & has_down)
            def _():
                for b in range(4):
                    up_far(b, relay_up.at[b], place(0, b, 0)).wait_recv()
                    for q in range(1, 4):
                        up_last(b, q).wait_recv()

        @pl.when(side == 1)
        def _():
            @pl.when(x < 3)
            def _():
                for b in range(4):
                    down_near(b).wait_recv()

            @pl.when((x == 3) & has_up)
            def _():
                for b in range(4):
                    down_far(b, relay_down.at[b], place(2, b, 3)).wait_recv()
                    for q in range(3):
                        down_last(b, q).wait_recv()

    def side_part(p, side):
        for j in range(3):
            query_start = j * QB + side * (2 * QB - 2 * j * QB)
            key_start = j * QB + side * (2 * RUN - j * QB)
            attend(p, query_start, key_start, RUN - j * QB, False)

    first_side = 1 - (x + 3) // 4
    for k in (1, 2, 3):
        out_y(k).wait_recv()
    out_core().start()
    wait_side(first_side)

    def early_part(p, carry):
        side_part(p, first_side)
        return carry

    lax.fori_loop(0, 3, early_part, 0)
    last_side = 1 - first_side
    wait_side(last_side)

    def ctx_copy(p, to, heads):
        return copy(
            context.at[pl.ds(to * ROWS, ROWS), pl.ds(pl.multiple_of(p * 128, 128), 128)],
            gathered.at[:, pl.ds(pl.multiple_of(heads * WIDTH + p * 128, 128), 128)],
            ctx_send.at[p, to], ctx_recv.at[p, heads], (utterance, seq, to),
        )

    def keeps(to):
        return is_near & (head == to)

    def late_part(p, carry):
        side_part(p, last_side)
        lanes = pl.ds(pl.multiple_of(p * 128, 128), 128)
        for j in range(3):
            rows = pl.ds(j * QB, QB)
            low, high = acc[p * 2, rows, :], acc[p * 2 + 1, rows, :]
            context[rows, lanes] = jnp.where(
                low_half, low[:, :128] / low[:, 128:], high[:, :128] / high[:, 128:]
            ).astype(jnp.bfloat16)
        for to in range(4):
            pl.when(jnp.logical_not(keeps(to)))(lambda: ctx_copy(p, to, group_of_heads).start())
        return carry

    lax.fori_loop(0, 3, late_part, 0)

    @pl.when(is_near)
    def _():
        own_lanes = pl.ds(pl.multiple_of(head * WIDTH, 128), WIDTH)
        gathered[:, own_lanes] = context[pl.ds(pl.multiple_of(head * ROWS, ROWS), ROWS), :]

    swap_marks().wait_send()
    for i, ref in enumerate((w_query, w_key, w_value)):
        weight_far(i, ref).wait_send()

    @pl.when(jnp.logical_not(is_near))
    def _():
        for i, ref in enumerate((w_query, w_key, w_value)):
            weight_there(i, ref).wait_send()
        for core in range(2):
            for k in (1, 2, 3):
                weight_line(core, k).wait_send()
                weight_plane(core, k).wait_send()

    pl.when(place_on_line > 0)(lambda: to_onward(head).wait_send())
    pl.when(place_on_line == 0)(lambda: to_back().wait_send())
    pl.when(place_on_line == 2)(lambda: to_onward(3 * utterance).wait_send())

    @pl.when(place_on_line == 1)
    def _():
        for t in (2, 3):
            to_onward(nth(t)).wait_send()

    for b in range(4):
        pl.when(is_near)(lambda: to_core(b).wait_send())
        pl.when(x < 3)(lambda: up_near(b).wait_send())
        pl.when(x > 0)(lambda: down_near(b).wait_send())

        @pl.when((x == 3) & has_up)
        def _():
            for q in range(3):
                up_spread(b, q).wait_send()

        @pl.when((x == 0) & has_down)
        def _():
            for q in range(1, 4):
                down_spread(b, q).wait_send()

        pl.when(has_up)(lambda: up_far(b, relay_up.at[b], landed_up.at[b]).wait_send())
        pl.when(has_down)(lambda: down_far(b, relay_down.at[b], landed_down.at[b]).wait_send())
        pl.when((x > 0) & has_down)(lambda: up_last(b, x).wait_send())
        pl.when((x < 3) & has_up)(lambda: down_last(b, x).wait_send())
    for k in (1, 2, 3):
        out_z(k).wait_send()
        out_x(k).wait_send()
        out_y(k).wait_send()
    out_core().wait()
    total = jnp.zeros((ROWS, D), jnp.float32)
    for g in range(4):
        for p in range(3):
            pl.when(jnp.logical_not(keeps(g)))(lambda: ctx_copy(p, g, g).wait_recv())
        total += jnp.dot(
            gathered[:, g * WIDTH:(g + 1) * WIDTH], projection[g], preferred_element_type=jnp.float32
        )
    out[...] = total.astype(jnp.bfloat16)
    for p in range(3):
        for to in range(4):
            pl.when(jnp.logical_not(keeps(to)))(lambda: ctx_copy(p, to, group_of_heads).wait_send())


def exchange_and_attend(frames, gain, w_query, w_key, w_value, w_out, marks):
    vmem, anywhere = (pl.BlockSpec(memory_space=m) for m in (pltpu.VMEM, pl.ANY))
    dma = pltpu.SemaphoreType.DMA
    bf16, f32 = jnp.bfloat16, jnp.float32
    return pl.pallas_call(
        kernel,
        out_shape=jax.ShapeDtypeStruct((ROWS, D), bf16),
        in_specs=[vmem, vmem, anywhere, anywhere, anywhere, anywhere, vmem],
        out_specs=vmem,
        scratch_shapes=[
            pltpu.VMEM((D, 3 * WIDTH), bf16),
            pltpu.VMEM((8, ROWS, D), bf16),
            pltpu.VMEM((16, 128), jnp.int32),
            pltpu.VMEM((RUN, WIDTH), bf16),
            pltpu.VMEM((3 * RUN, 2 * WIDTH), bf16),
            pltpu.VMEM((3 * RUN, 128), bf16),
            pltpu.VMEM((RUN, 128), bf16),
            pltpu.VMEM((6, RUN, 256), f32),
            pltpu.VMEM((6, RUN, 128), f32),
            pltpu.VMEM((RUN, WIDTH), bf16),
            pltpu.VMEM((ROWS, D), bf16),
            pltpu.VMEM((4, PIECE, 2 * WIDTH), bf16),
            pltpu.VMEM((4, PIECE, 2 * WIDTH), bf16),
            pltpu.VMEM((4, PIECE, 2 * WIDTH), bf16),
            pltpu.VMEM((4, PIECE, 2 * WIDTH), bf16),
            pltpu.VMEM((4, WIDTH, D), bf16),
            dma, dma, dma((3,)), dma((3,)), dma((3,)),
            dma((3,)), dma((2, 3)), dma((2, 3)), dma((2, 3)), dma((2, 3)), dma((2, 3)),
            dma((4,)), dma, dma((4,)), dma((4,)), dma((4,)),
            dma((4,)), dma((4,)), dma((4,)), dma((4,)),
            dma((4, 4)), dma((4,)), dma((4, 4)), dma((4,)),
            dma((4,)), dma((4,)), dma((4,)), dma((4,)),
            dma((4,)), dma((4, 4)), dma((4,)), dma((4, 4)),
            dma((3, 4)), dma((3, 4)),
            dma, dma((3,)), dma((3,)), dma((3,)), dma((3,)), dma((3,)), dma((3,)), dma, dma,
        ],
        compiler_params=pltpu.CompilerParams(
            collective_id=0, has_side_effects=True, vmem_limit_bytes=63 * 2**20
        ),
        cost_estimate=pl.CostEstimate(flops=60_000_000_000, bytes_accessed=8_000_000, transcendentals=8_000_000),
        name="attend",
    )(frames, gain, w_query, w_key, w_value, w_out, marks)


def local(frames, norm_gain, w_query, w_key, w_value, w_out, group_band, lengths):
    band = jnp.pad(group_band[0].T, ((0, 4), (0, 128 - REACH)))
    marks = jnp.where(lax.broadcasted_iota(jnp.int32, (16, 128), 0) == 12, lengths[0], band)
    update = exchange_and_attend(frames[0], norm_gain, w_query, w_key, w_value, w_out, marks)
    return update[None]


def solution(mesh):
    return jax.shard_map(
        local,
        mesh=mesh,
        in_specs=(
            P("dp", ("seq", "head"), None),
            P(),
            P("dp", "head"),
            P("dp", "head"),
            P("dp", "head"),
            P("head", "dp"),
            P("dp", "seq", None),
            P("dp"),
        ),
        out_specs=P("dp", ("seq", "head"), None),
        check_vma=False,
    )
```

```python
import functools

import jax
import jax.numpy as jnp
from jax import lax
from jax.experimental import pallas as pl
from jax.experimental.pallas import tpu as pltpu
from jax.sharding import PartitionSpec as P

MESH = pl.DeviceIdType.MESH
HD = 64
GROUP = 128
ROWS = 192
RUN = 768
WIDTH = 384
D = 1536
REACH = 6
PIECE = 48
QB = 256
FORBIDDEN = -1e30
epsilon = 1e-05


def kernel(
    frames, gain, w_query, w_key, w_value, w_out, marks, out,
    weights, normalized, other_marks, query, kv, bias, onehot, acc, top, context, gathered, relay_up, relay_down, landed_up, landed_down, projection,
    marks_send, marks_recv, w_send, w_recv, w_local, far_w_send, far_w_recv, line_w_send, line_w_recv, plane_w_send, plane_w_recv,
    on_send, out_send, block_recv, core_send, core_recv,
    up_send, up_recv, down_send, down_recv,
    spread_up_send, spread_up_recv, spread_down_send, spread_down_recv,
    far_up_send, far_up_recv, far_down_send, far_down_recv,
    last_up_send, last_up_recv, last_down_send, last_down_recv,
    ctx_send, ctx_recv,
    out_local, out_z_send, out_z_recv, out_x_send, out_x_recv, out_y_send, out_y_recv, out_core_send, out_core_recv,
):
    dp, seq, head = lax.axis_index("dp"), lax.axis_index("seq"), lax.axis_index("head")
    row, x = seq // 4, seq % 4
    y = seq // 16
    utterance = head // 2
    near = 1 - (dp + utterance) % 2
    is_near = near == 1
    group_of_heads = (head + 2 * (1 - near)) % 4
    other_core = (1 - dp, seq, head)
    place_on_line = head + dp * (3 - 2 * head)
    first_seq = row * 4
    has_up, has_down = row < 15, row > 0

    def copy(src, dst, send, recv, to):
        return pltpu.make_async_remote_copy(
            src_ref=src, dst_ref=dst, send_sem=send, recv_sem=recv, device_id=to, device_id_type=MESH
        )

    barrier = pltpu.get_barrier_semaphore()

    def greet(to):
        pl.semaphore_signal(barrier, inc=1, device_id=to, device_id_type=MESH)

    greet(other_core)
    for k in (1, 2, 3):
        greet((dp, seq, (head + k) % 4))
        greet((1 - dp, seq, (head + k) % 4))
        greet((dp, first_seq + (x + k) % 4, head))
        greet((dp, (seq + 16 * k) % 64, head))

    pl.when(has_up)(lambda: greet((dp, (seq + 4) % 64, head)))
    pl.when(has_down)(lambda: greet((dp, (seq + 60) % 64, head)))
    pl.semaphore_wait(barrier, 13 + (1 - (row + 1) // 16) + (row + 15) // 16)

    def swap_marks():
        return copy(marks, other_marks, marks_send, marks_recv, other_core)

    swap_marks().start()

    half = pl.ds(pl.multiple_of(dp * (D // 2), D // 2), D // 2)

    def weight_there(i, ref):
        part = weights.at[half, pl.ds(i * WIDTH, WIDTH)]
        return copy(ref, part, w_send.at[i], w_recv.at[i], other_core)

    def weight_here(i, ref):
        return pltpu.make_async_copy(ref, weights.at[half, pl.ds(i * WIDTH, WIDTH)], w_local.at[i])

    first, second = (1 - dp) * y + dp * x, (1 - dp) * x + dp * y

    def weight_far(i, ref):
        start = first * ROWS + second * PIECE
        return copy(
            ref.at[pl.ds(pl.multiple_of(start, 16), PIECE), :],
            weights.at[pl.ds(pl.multiple_of(dp * (D // 2) + start, 16), PIECE), pl.ds(i * WIDTH, WIDTH)],
            far_w_send.at[i], far_w_recv.at[dp, i], (utterance, seq, (head + 2) % 4),
        )

    def weight_arrived(core, i, ref):
        return copy(
            ref.at[pl.ds(0, PIECE), :], weights.at[pl.ds(0, PIECE), pl.ds(i * WIDTH, WIDTH)],
            far_w_send.at[i], far_w_recv.at[core, i], other_core,
        )

    def over_x(k):
        return (dp, first_seq + (x + k) % 4, head)

    def over_y(k):
        return (dp, (seq + 16 * k) % 64, head)

    def weight_line(core, k):
        start = core * (D // 2) + (x * ROWS + y * PIECE if core else y * ROWS + x * PIECE)
        part = weights.at[pl.ds(pl.multiple_of(start, 16), PIECE), :]
        return copy(
            part, part, line_w_send.at[core, k - 1], line_w_recv.at[core, k - 1], over_y(k) if core else over_x(k)
        )

    def weight_plane(core, k):
        start = core * (D // 2) + (x if core else y) * ROWS
        part = weights.at[pl.ds(pl.multiple_of(start, 16), ROWS), :]
        return copy(
            part, part, plane_w_send.at[core, k - 1], plane_w_recv.at[core, k - 1], over_x(k) if core else over_y(k)
        )

    for i, ref in enumerate((w_query, w_key, w_value)):
        weight_far(i, ref).start()

        @pl.when(is_near)
        def _():
            weight_here(i, ref).start()

        @pl.when(jnp.logical_not(is_near))
        def _():
            weight_there(i, ref).start()

    piece_rows = pl.ds(pl.multiple_of(y * 96 + x % 2 * 48, 16), 48)
    strip_rows = pl.ds(pl.multiple_of(y * 96, 16), 96)
    piece_from = pl.ds(pl.multiple_of(x // 2 * WIDTH, 128), WIDTH)
    piece_columns = pl.ds(pl.multiple_of(dp * (D // 2) + x // 2 * WIDTH, 128), WIDTH)

    def out_here():
        return pltpu.make_async_copy(
            w_out.at[piece_rows, piece_from], projection.at[head, piece_rows, piece_columns], out_local
        )

    def out_z(k):
        return copy(
            w_out.at[piece_rows, piece_from], projection.at[head, piece_rows, piece_columns],
            out_z_send.at[k - 1], out_z_recv.at[k - 1], (dp, seq, (head + k) % 4),
        )

    def out_x(k):
        part = projection.at[:, piece_rows, piece_columns]
        return copy(part, part, out_x_send.at[k - 1], out_x_recv.at[k - 1], (dp, first_seq + (x + k) % 4, head))

    def out_y(k):
        part = projection.at[:, strip_rows, half]
        return copy(part, part, out_y_send.at[k - 1], out_y_recv.at[k - 1], (dp, (seq + 16 * k) % 64, head))

    def out_core():
        part = projection.at[:, :, half]
        return copy(part, part, out_core_send, out_core_recv, (1 - dp, seq, head))

    out_here().start()
    for k in (2, 1, 3):
        out_z(k).start()

    values = frames[...].astype(jnp.float32)
    center = values - jnp.mean(values, axis=-1, keepdims=True)
    spread = jnp.mean(center * center, axis=-1, keepdims=True)
    normalized[head] = (center * lax.rsqrt(spread + epsilon) * gain[...][None, :]).astype(jnp.bfloat16)

    step = 1 - 2 * dp
    onward = (dp, seq, (head + 4 - step) % 4)
    back = (dp, seq, (head + 4 + step) % 4)

    def to_onward(b):
        return copy(normalized.at[b], normalized.at[b], on_send.at[b], block_recv.at[b], onward)

    def to_back():
        return copy(normalized.at[head], normalized.at[head], out_send, block_recv.at[head], back)

    def to_core(b):
        return copy(normalized.at[b], normalized.at[4 + b], core_send.at[b], core_recv.at[b], other_core)

    pl.when(place_on_line > 0)(lambda: to_onward(head).start())
    pl.when(place_on_line == 0)(lambda: to_back().start())

    onehot[...] = (
        lax.broadcasted_iota(jnp.int32, (RUN, 128), 0) // GROUP
        == lax.broadcasted_iota(jnp.int32, (RUN, 128), 1)
    ).astype(jnp.bfloat16)
    swap_marks().wait_recv()
    seen_marks = marks[...] * near + other_marks[...] * (1 - near)
    length = seen_marks[12:13, :]
    lane = lax.broadcasted_iota(jnp.int32, (1, 128), 1)
    within = lax.broadcasted_iota(jnp.int32, (GROUP, 128), 0)
    for kg in range(3 * REACH):
        seen = jnp.zeros((1, 128), jnp.int32)
        own = jnp.zeros((1, 128), jnp.int32)
        for g in range(REACH):
            offset = kg - REACH - g
            if offset == 0:
                own = jnp.where(lane == g, 1, own)
            elif abs(offset) <= REACH:
                column = offset + REACH if offset < 0 else offset + REACH - 1
                seen = jnp.where(lane == g, seen_marks[column:column + 1, :], seen)
        group = seq * REACH - REACH + kg
        inside = jnp.where((group >= 0) & (group < 64 * REACH), 1, 0)
        alive = (group * GROUP + within < length).astype(jnp.int32) * inside
        allowed = (jnp.where(seen == 1, 1, 0) * alive + own) > 0
        bias[kg * GROUP:(kg + 1) * GROUP, :] = jnp.where(allowed, 0.0, FORBIDDEN).astype(jnp.bfloat16)

    @pl.when(seq == 0)
    def _():
        kv[0:RUN, :] = jnp.zeros((RUN, 2 * WIDTH), jnp.bfloat16)

    @pl.when(seq == 63)
    def _():
        kv[2 * RUN:3 * RUN, :] = jnp.zeros((RUN, 2 * WIDTH), jnp.bfloat16)

    def spread_out_weights():
        out_here().wait()
        for k in (1, 2, 3):
            out_z(k).wait_recv()
        for k in (2, 1, 3):
            out_x(k).start()

    @pl.when(is_near)
    def _():
        for i, ref in enumerate((w_query, w_key, w_value)):
            weight_here(i, ref).wait()
            weight_there(i, ref).wait_recv()
        spread_out_weights()

    @pl.when(jnp.logical_not(is_near))
    def _():
        for core in range(2):
            for i, ref in enumerate((w_query, w_key, w_value)):
                weight_arrived(core, i, ref).wait_recv()
            for k in (2, 1, 3):
                weight_line(core, k).start()
        spread_out_weights()
        for core in range(2):
            for k in (1, 2, 3):
                weight_line(core, k).wait_recv()
            for k in (2, 1, 3):
                weight_plane(core, k).start()

        @pl.when(place_on_line == 2)
        def _():
            to_onward(3 * utterance).wait_recv()
            to_onward(3 * utterance).start()

        for k in (1, 2, 3):
            out_x(k).wait_recv()
        for k in (2, 1, 3):
            out_y(k).start()
        for core in range(2):
            for k in (1, 2, 3):
                weight_plane(core, k).wait_recv()

    def place(side, b, q=None):
        start, size = side * RUN + b * ROWS, ROWS
        if q is not None:
            start, size = start + q * PIECE, PIECE
        return kv.at[pl.ds(pl.multiple_of(start, 16), size), :]

    def up_near(b):
        return copy(place(1, b), place(0, b), up_send.at[b], up_recv.at[b], (dp, (seq + 1) % 64, head))

    def down_near(b):
        return copy(place(1, b), place(2, b), down_send.at[b], down_recv.at[b], (dp, (seq + 63) % 64, head))

    def up_spread(b, q):
        return copy(
            place(1, b, q), relay_up.at[b], spread_up_send.at[b, q], spread_up_recv.at[b], (dp, first_seq + q, head)
        )

    def down_spread(b, q):
        return copy(
            place(1, b, q), relay_down.at[b], spread_down_send.at[b, q], spread_down_recv.at[b],
            (dp, first_seq + q, head),
        )

    def up_far(b, src, dst):
        return copy(src, dst, far_up_send.at[b], far_up_recv.at[b], (dp, (seq + 4) % 64, head))

    def down_far(b, src, dst):
        return copy(src, dst, far_down_send.at[b], far_down_recv.at[b], (dp, (seq + 60) % 64, head))

    def up_last(b, q):
        return copy(
            landed_up.at[b], place(0, b, q), last_up_send.at[b], last_up_recv.at[b, q], (dp, first_seq, head)
        )

    def down_last(b, q):
        return copy(
            landed_down.at[b], place(2, b, q), last_down_send.at[b], last_down_recv.at[b, q],
            (dp, first_seq + 3, head),
        )

    def send_near(b):
        pl.when(x < 3)(lambda: up_near(b).start())
        pl.when(x > 0)(lambda: down_near(b).start())

    def send_block(b):
        @pl.when((x == 3) & has_up)
        def _():
            for q in range(3):
                up_spread(b, q).start()

        @pl.when((x == 0) & has_down)
        def _():
            for q in range(1, 4):
                down_spread(b, q).start()

    def relay_block(b):
        @pl.when(has_up)
        def _():
            pl.when(x < 3)(lambda: up_spread(b, x).wait_recv())
            pl.when(x == 0)(lambda: up_far(b, relay_up.at[b], place(0, b, 0)).start())
            pl.when((x > 0) & (x < 3))(lambda: up_far(b, relay_up.at[b], landed_up.at[b]).start())
            pl.when(x == 3)(lambda: up_far(b, place(1, b, 3), landed_up.at[b]).start())

        @pl.when(has_down)
        def _():
            pl.when(x > 0)(lambda: down_spread(b, x).wait_recv())
            pl.when(x == 3)(lambda: down_far(b, relay_down.at[b], place(2, b, 3)).start())
            pl.when((x > 0) & (x < 3))(lambda: down_far(b, relay_down.at[b], landed_down.at[b]).start())
            pl.when(x == 0)(lambda: down_far(b, place(1, b, 0), landed_down.at[b]).start())

    def deliver_block(b):
        @pl.when((x > 0) & has_down)
        def _():
            up_far(b, relay_up.at[b], landed_up.at[b]).wait_recv()
            up_last(b, x).start()

        @pl.when((x < 3) & has_up)
        def _():
            down_far(b, relay_down.at[b], landed_down.at[b]).wait_recv()
            down_last(b, x).start()

    far_end = head // 2
    mirrored = head + far_end * (3 - 2 * head)

    def nth(t):
        near = t // 2 * 2 + (t + mirrored * (1 - t // 2)) % 2
        return near + far_end * (3 - 2 * near)

    def project(t, carry):
        b = nth(t)

        @pl.when(is_near)
        def _():
            pl.when(t > 0)(lambda: to_onward(b).wait_recv())
            pl.when((place_on_line == 1) & (t > 1))(lambda: to_onward(b).start())
            to_core(b).start()

        @pl.when(jnp.logical_not(is_near))
        def _():
            to_core(b).wait_recv()

        @pl.when(is_near & (t == 1))
        def _():
            for k in (1, 2, 3):
                out_x(k).wait_recv()
            for k in (2, 1, 3):
                out_y(k).start()

        rows = normalized[b + 4 * (1 - near)]
        product = jnp.dot(rows, weights[...], preferred_element_type=jnp.float32).astype(jnp.bfloat16)
        start = pl.multiple_of(b * ROWS, ROWS)
        query[pl.ds(start, ROWS), :] = product[:, :WIDTH] * jnp.bfloat16(0.125)
        kv[pl.ds(pl.multiple_of(RUN + start, ROWS), ROWS), :] = product[:, WIDTH:]
        send_block(b)
        pl.when(is_near)(lambda: send_near(b))
        return carry

    lax.fori_loop(0, 4, project, 0)

    def relay(t, carry):
        relay_block(nth(t))
        return carry

    @pl.when(jnp.logical_not(is_near))
    def _():
        for t in range(4):
            send_near(nth(t))

    lax.fori_loop(0, 4, relay, 0)

    low_half = lax.broadcasted_iota(jnp.int32, (QB, 128), 1) < HD

    def attend(p, query_start, key_start, keys, first):
        lanes = pl.ds(pl.multiple_of(p * 128, 128), 128)
        value_lanes = pl.ds(pl.multiple_of(WIDTH + p * 128, 128), 128)
        key_rows = pl.ds(pl.multiple_of(key_start, QB), keys)
        query_rows = pl.ds(pl.multiple_of(query_start, QB), QB)
        key_tile = jnp.concatenate([kv[key_rows, lanes], bias[key_rows, :]], axis=1)
        value_tile = jnp.concatenate([kv[key_rows, value_lanes], jnp.ones((keys, 128), jnp.bfloat16)], axis=1)
        query_tile = query[query_rows, lanes]
        marks = onehot[query_rows, :]
        for hh in range(2):
            h = p * 2 + hh
            mine = jnp.where(low_half == (hh == 0), query_tile, jnp.zeros_like(query_tile))
            scores = lax.dot_general(
                jnp.concatenate([mine, marks], axis=1), key_tile, (((1,), (1,)), ((), ())),
                preferred_element_type=jnp.float32,
            )
            here = jnp.max(scores, axis=-1, keepdims=True)
            if first:
                best = here
            else:
                before = top[h, query_rows, :][:, :1]
                best = jnp.maximum(before, here)
            rounded = jnp.exp(scores - best).astype(jnp.bfloat16)
            part = jnp.dot(rounded, value_tile, preferred_element_type=jnp.float32)
            if not first:
                part = part + acc[h, query_rows, :] * jnp.exp(before - best)
            acc[h, query_rows, :] = part
            top[h, query_rows, :] = jnp.broadcast_to(best, (QB, 128))

    def own_part(p, carry):
        for j in range(3):
            attend(p, j * QB, RUN, RUN, True)

        @pl.when(p == 0)
        def _():
            deliver_block(nth(0))
            deliver_block(nth(1))

        pl.when(p > 0)(lambda: deliver_block(nth(p + 1)))
        return carry

    lax.fori_loop(0, 3, own_part, 0)

    def wait_side(side):
        @pl.when(side == 0)
        def _():
            @pl.when(x > 0)
            def _():
                for b in range(4):
                    up_near(b).wait_recv()

            @pl.when((x == 0) & has_down)
            def _():
                for b in range(4):
                    up_far(b, relay_up.at[b], place(0, b, 0)).wait_recv()
                    for q in range(1, 4):
                        up_last(b, q).wait_recv()

        @pl.when(side == 1)
        def _():
            @pl.when(x < 3)
            def _():
                for b in range(4):
                    down_near(b).wait_recv()

            @pl.when((x == 3) & has_up)
            def _():
                for b in range(4):
                    down_far(b, relay_down.at[b], place(2, b, 3)).wait_recv()
                    for q in range(3):
                        down_last(b, q).wait_recv()

    def side_part(p, side):
        for j in range(3):
            query_start = j * QB + side * (2 * QB - 2 * j * QB)
            key_start = j * QB + side * (2 * RUN - j * QB)
            attend(p, query_start, key_start, RUN - j * QB, False)

    first_side = 1 - (x + 3) // 4
    for k in (1, 2, 3):
        out_y(k).wait_recv()
    out_core().start()
    wait_side(first_side)

    def early_part(p, carry):
        side_part(p, first_side)
        return carry

    lax.fori_loop(0, 3, early_part, 0)
    last_side = 1 - first_side
    wait_side(last_side)

    def ctx_copy(p, to, heads):
        return copy(
            context.at[pl.ds(pl.multiple_of(to * ROWS, ROWS), ROWS), pl.ds(pl.multiple_of(p * 128, 128), 128)],
            gathered.at[:, pl.ds(pl.multiple_of(heads * WIDTH + p * 128, 128), 128)],
            ctx_send.at[p, to], ctx_recv.at[p, heads], (utterance, seq, to),
        )

    def keeps(to):
        return is_near & (head == to)

    def late_part(p, carry):
        side_part(p, last_side)
        lanes = pl.ds(pl.multiple_of(p * 128, 128), 128)
        for j in range(3):
            rows = pl.ds(j * QB, QB)
            low, high = acc[p * 2, rows, :], acc[p * 2 + 1, rows, :]
            context[rows, lanes] = jnp.where(
                low_half, low[:, :128] / low[:, 128:], high[:, :128] / high[:, 128:]
            ).astype(jnp.bfloat16)
        for n in range(4):
            to = 3 - n + utterance * (2 * n - 3)
            pl.when(jnp.logical_not(keeps(to)))(lambda: ctx_copy(p, to, group_of_heads).start())
        return carry

    lax.fori_loop(0, 3, late_part, 0)

    @pl.when(is_near)
    def _():
        own_lanes = pl.ds(pl.multiple_of(head * WIDTH, 128), WIDTH)
        gathered[:, own_lanes] = context[pl.ds(pl.multiple_of(head * ROWS, ROWS), ROWS), :]

    swap_marks().wait_send()
    for i, ref in enumerate((w_query, w_key, w_value)):
        weight_far(i, ref).wait_send()

    @pl.when(jnp.logical_not(is_near))
    def _():
        for i, ref in enumerate((w_query, w_key, w_value)):
            weight_there(i, ref).wait_send()
        for core in range(2):
            for k in (1, 2, 3):
                weight_line(core, k).wait_send()
                weight_plane(core, k).wait_send()

    pl.when(place_on_line > 0)(lambda: to_onward(head).wait_send())
    pl.when(place_on_line == 0)(lambda: to_back().wait_send())
    pl.when(place_on_line == 2)(lambda: to_onward(3 * utterance).wait_send())

    @pl.when(place_on_line == 1)
    def _():
        for t in (2, 3):
            to_onward(nth(t)).wait_send()

    for b in range(4):
        pl.when(is_near)(lambda: to_core(b).wait_send())
        pl.when(x < 3)(lambda: up_near(b).wait_send())
        pl.when(x > 0)(lambda: down_near(b).wait_send())

        @pl.when((x == 3) & has_up)
        def _():
            for q in range(3):
                up_spread(b, q).wait_send()

        @pl.when((x == 0) & has_down)
        def _():
            for q in range(1, 4):
                down_spread(b, q).wait_send()

        pl.when(has_up)(lambda: up_far(b, relay_up.at[b], landed_up.at[b]).wait_send())
        pl.when(has_down)(lambda: down_far(b, relay_down.at[b], landed_down.at[b]).wait_send())
        pl.when((x > 0) & has_down)(lambda: up_last(b, x).wait_send())
        pl.when((x < 3) & has_up)(lambda: down_last(b, x).wait_send())
    for k in (1, 2, 3):
        out_z(k).wait_send()
        out_x(k).wait_send()
        out_y(k).wait_send()
    out_core().wait()
    total = jnp.zeros((ROWS, D), jnp.float32)
    for g in range(4):
        for p in range(3):
            pl.when(jnp.logical_not(keeps(g)))(lambda: ctx_copy(p, g, g).wait_recv())
        total += jnp.dot(
            gathered[:, g * WIDTH:(g + 1) * WIDTH], projection[g], preferred_element_type=jnp.float32
        )
    out[...] = total.astype(jnp.bfloat16)
    for p in range(3):
        for to in range(4):
            pl.when(jnp.logical_not(keeps(to)))(lambda: ctx_copy(p, to, group_of_heads).wait_send())


def exchange_and_attend(frames, gain, w_query, w_key, w_value, w_out, marks):
    vmem, anywhere = (pl.BlockSpec(memory_space=m) for m in (pltpu.VMEM, pl.ANY))
    dma = pltpu.SemaphoreType.DMA
    bf16, f32 = jnp.bfloat16, jnp.float32
    return pl.pallas_call(
        kernel,
        out_shape=jax.ShapeDtypeStruct((ROWS, D), bf16),
        in_specs=[vmem, vmem, anywhere, anywhere, anywhere, anywhere, vmem],
        out_specs=vmem,
        scratch_shapes=[
            pltpu.VMEM((D, 3 * WIDTH), bf16),
            pltpu.VMEM((8, ROWS, D), bf16),
            pltpu.VMEM((16, 128), jnp.int32),
            pltpu.VMEM((RUN, WIDTH), bf16),
            pltpu.VMEM((3 * RUN, 2 * WIDTH), bf16),
            pltpu.VMEM((3 * RUN, 128), bf16),
            pltpu.VMEM((RUN, 128), bf16),
            pltpu.VMEM((6, RUN, 256), f32),
            pltpu.VMEM((6, RUN, 128), f32),
            pltpu.VMEM((RUN, WIDTH), bf16),
            pltpu.VMEM((ROWS, D), bf16),
            pltpu.VMEM((4, PIECE, 2 * WIDTH), bf16),
            pltpu.VMEM((4, PIECE, 2 * WIDTH), bf16),
            pltpu.VMEM((4, PIECE, 2 * WIDTH), bf16),
            pltpu.VMEM((4, PIECE, 2 * WIDTH), bf16),
            pltpu.VMEM((4, WIDTH, D), bf16),
            dma, dma, dma((3,)), dma((3,)), dma((3,)),
            dma((3,)), dma((2, 3)), dma((2, 3)), dma((2, 3)), dma((2, 3)), dma((2, 3)),
            dma((4,)), dma, dma((4,)), dma((4,)), dma((4,)),
            dma((4,)), dma((4,)), dma((4,)), dma((4,)),
            dma((4, 4)), dma((4,)), dma((4, 4)), dma((4,)),
            dma((4,)), dma((4,)), dma((4,)), dma((4,)),
            dma((4,)), dma((4, 4)), dma((4,)), dma((4, 4)),
            dma((3, 4)), dma((3, 4)),
            dma, dma((3,)), dma((3,)), dma((3,)), dma((3,)), dma((3,)), dma((3,)), dma, dma,
        ],
        compiler_params=pltpu.CompilerParams(
            collective_id=0, has_side_effects=True, vmem_limit_bytes=63 * 2**20
        ),
        cost_estimate=pl.CostEstimate(flops=60_000_000_000, bytes_accessed=8_000_000, transcendentals=8_000_000),
        name="attend",
    )(frames, gain, w_query, w_key, w_value, w_out, marks)


def local(frames, norm_gain, w_query, w_key, w_value, w_out, group_band, lengths):
    band = jnp.pad(group_band[0].T, ((0, 4), (0, 128 - REACH)))
    marks = jnp.where(lax.broadcasted_iota(jnp.int32, (16, 128), 0) == 12, lengths[0], band)
    update = exchange_and_attend(frames[0], norm_gain, w_query, w_key, w_value, w_out, marks)
    return update[None]


def solution(mesh):
    return jax.shard_map(
        local,
        mesh=mesh,
        in_specs=(
            P("dp", ("seq", "head"), None),
            P(),
            P("dp", "head"),
            P("dp", "head"),
            P("dp", "head"),
            P("head", "dp"),
            P("dp", "seq", None),
            P("dp"),
        ),
        out_specs=P("dp", ("seq", "head"), None),
        check_vma=False,
    )
```
